256 devices in a mesh: illum: 32 (over x, z), slab: 8 (over y, core).
Axes of the slice: x: 4, y: 4, z: 8, core: 2. Of those that a mesh axis runs over, the one named last changes fastest.
Arguments:
- angles: int32 [32, 2], P('illum'), may hold values from -16 to 16
- contrast: float32 [8, 256, 256], P('slab', 'illum'), may hold values from 0.003 to 0.15
- measured: float32 [32, 2, 256, 256], P('illum'), may hold values from -3.2 to 3.2
Outputs:
- fields: float32 [32, 2, 8, 256, 256], P('illum', None, 'slab')
- descent: float32 [8, 256, 256], P('slab', 'illum')
- misfit: float32 [], replicated
The draws below stay inside these ranges and needn't reach their ends.
All inputs are finite; a program needn't handle non-finite values.
Results may differ from the reference program's by a relative error of at most 0.0003.
Values sent between devices are 32-bit elements; how exact they have to be, the bound alone decides.
A program may use at most 64 MiB of HBM per device.

```python
import math
import jax
import jax.numpy as jnp
from jax import lax

NX = 256
NY = 256
ITERS = 2
NZ = 8
ILLUMS = 32


def draw_contrast(key, part):
    key = jax.random.fold_in(key, 11)
    cell_key, row_key = jax.random.split(key, 2)
    cells = jax.random.uniform(cell_key, (NZ, NX, NY), jnp.float32, 0.2, 1.0)
    row_scale = jnp.exp(-math.log(10.0) * jax.random.uniform(row_key, (NZ, NX, 1), jnp.float32))
    return 0.15 * row_scale * cells


def draw_measured(key, part):
    key = jax.random.fold_in(key, 23)
    base_key = jax.random.fold_in(key, 0)
    ordering = jnp.arange(ILLUMS, dtype=jnp.int32).astype(jnp.float32) / max(ILLUMS - 1, 1)
    scales = 0.3 * (1.0 + 2.0 * ordering)
    values = jnp.clip(jax.random.normal(base_key, (ILLUMS, 2, NX, NY), jnp.float32), -3.5, 3.5)
    return values * scales[:, None, None, None]


def with_ends(values, own_key, low, high):
    place = [jax.random.randint(jax.random.fold_in(own_key, axis), (), 0, length) for axis, length in enumerate(values.shape)]
    main_axis = values.shape.index(max(values.shape))
    beside = place[:main_axis] + [(place[main_axis] + 1) % values.shape[main_axis]] + place[main_axis + 1:]
    return values.at[tuple(place)].set(low).at[tuple(beside)].set(high)


def setup_inputs(seed: int = 0) -> dict:
    streams_of = jax.random.split(jax.random.key(seed), 4)
    return {
        "angles": with_ends(jax.random.randint(streams_of[0], (ILLUMS, 2), -16, 17), jax.random.fold_in(streams_of[0], 1), -16, 16).astype(jnp.int32),
        "contrast": draw_contrast(jax.random.fold_in(streams_of[3], 71), 0),
        "measured": draw_measured(jax.random.fold_in(streams_of[3], 71), 0),
    }


wave_number = 2.0 * math.pi / 8.0
damping = 0.2
tilt_step = 0.04

def symbol(indices, length):
    return 2.0 - 2.0 * jnp.cos(2.0 * math.pi / length * indices.astype(jnp.float32))

def depth_kernel(distance, transverse):
    squared = wave_number * wave_number
    shifted = transverse - squared
    loss_term = squared * damping
    radius = jnp.sqrt(shifted * shifted + loss_term * loss_term)
    decay_rate = jnp.sqrt(0.5 * (radius + shifted))
    turn_rate = jnp.sqrt(0.5 * (radius - shifted))
    scale = squared / (2.0 * radius) * jnp.exp(-decay_rate * distance)
    cosine_part = jnp.cos(turn_rate * distance)
    sine_part = jnp.sin(turn_rate * distance)
    return (scale * (decay_rate * cosine_part - turn_rate * sine_part), -scale * (decay_rate * sine_part + turn_rate * cosine_part))

def squared_norm(values):
    return jnp.sum(jnp.real(values) * jnp.real(values) + jnp.imag(values) * jnp.imag(values))

def reference(angles, contrast, measured):
    wave_z = jnp.arange(NZ, dtype=jnp.int32)
    wave_x = jnp.arange(NX, dtype=jnp.int32)
    wave_y = jnp.arange(NY, dtype=jnp.int32)
    transverse = symbol(wave_x, NX)[:, None] + symbol(wave_y, NY)[None, :]
    kernel_real, kernel_imaginary = depth_kernel(wave_z.astype(jnp.float32)[:, None, None], transverse[None])
    kernel = kernel_real + 1j * kernel_imaginary
    kernel_conj = jnp.conj(kernel)
    z_position = wave_z.astype(jnp.float32)
    x_coordinate = wave_x.astype(jnp.float32)
    y_position = wave_y.astype(jnp.float32)

    def convolve(values, table):
        spectrum = jnp.fft.fft2(values, axes=(1, 2))

        def one_plane(plane_index):
            distance = jnp.abs(plane_index - wave_z).astype(jnp.int32)
            return lax.optimization_barrier(jnp.sum(table[distance] * spectrum, axis=0))
        summed = lax.map(one_plane, wave_z)
        return jnp.fft.ifft2(summed, axes=(1, 2))

    def forward(values):
        return values - convolve(contrast * values, kernel)

    def adjoint(values):
        return values - contrast * convolve(values, kernel_conj)

    def per_illumination(running, inputs):
        grad_sum, misfit_sum = running
        tilt_index, observed = inputs
        tilts = jnp.sin(tilt_step * tilt_index.astype(jnp.float32))
        sine_x = tilts[0]
        sine_y = tilts[1]
        cosine_z = jnp.sqrt(1.0 - sine_x * sine_x - sine_y * sine_y)
        phases = wave_number * (sine_x * x_coordinate[None, :, None] + sine_y * y_position[None, None, :] + cosine_z * z_position[:, None, None])
        incident = jnp.cos(phases) + 1j * jnp.sin(phases)
        solution = incident
        residual = convolve(contrast * incident, kernel)
        gradient_dir = adjoint(residual)
        direction = gradient_dir
        norm_now = squared_norm(gradient_dir)
        for iteration in range(ITERS):
            mapped = forward(direction)
            step_size = norm_now / squared_norm(mapped)
            solution = solution + step_size * direction
            residual = residual - step_size * mapped
            gradient_dir = adjoint(residual)
            norm_next = squared_norm(gradient_dir)
            direction = gradient_dir + norm_next / norm_now * direction
            norm_now = norm_next
        mismatch = solution[NZ - 1] - incident[NZ - 1] - (observed[0] + 1j * observed[1])
        misfit = 0.5 * squared_norm(mismatch)
        source_field = jnp.zeros_like(solution).at[NZ - 1].set(mismatch)
        back_field = convolve(source_field, kernel_conj)
        partial_value = jnp.real(solution) * jnp.real(back_field) + jnp.imag(solution) * jnp.imag(back_field)
        stacked = jnp.stack([jnp.real(solution), jnp.imag(solution)])
        return ((grad_sum + partial_value, misfit_sum + misfit), stacked)
    initial = (jnp.zeros((NZ, NX, NY), jnp.float32), jnp.zeros((), jnp.float32))
    (gradient, misfit), fields = lax.scan(per_illumination, initial, (angles, measured))
    mean_square = jnp.sum(gradient * gradient) / (NZ * NX * NY)
    descent = gradient / jnp.sqrt(mean_square + 1e-06)
    return (fields, descent, misfit)
```

```python
import functools
import math

import jax
import jax.numpy as jnp
import ml_dtypes
import numpy as np
from jax import lax
from jax.experimental import pallas as pl
from jax.experimental.pallas import tpu as pltpu
from jax.sharding import PartitionSpec as P

MESH = pl.DeviceIdType.MESH
N = 256
H = 128
NZ = 8
ILLUMS = 32
WAVE = 2.0 * math.pi / 8.0
DAMPING = 0.2
TILT = 0.04
CHUNKS = 4
CR = 64


def split_np(m):
    hi = m.astype(ml_dtypes.bfloat16)
    lo = (m - hi.astype(np.float64)).astype(ml_dtypes.bfloat16)
    return np.stack([hi, lo])


def dft_tables():
    n = np.arange(H)[:, None]
    m = np.arange(H)[None, :]
    out = []
    for q in (0, 1):
        theta = -2.0 * np.pi / N * ((n * (2 * m + q)) % N)
        c, s = np.cos(theta), np.sin(theta)
        out.append(np.block([[c, s], [-s, c]]))
    right = np.stack([split_np(r) for r in out])
    left = np.stack([split_np(np.ascontiguousarray(r.T)) for r in out])
    return right, left


def depth_tables():
    order = np.concatenate([np.arange(0, N, 2), np.arange(1, N, 2)])
    sym = 2.0 - 2.0 * np.cos(2.0 * np.pi / N * order)
    b = WAVE * WAVE
    p = sym[:, None] + sym[None, :] - b
    l = b * DAMPING
    r = np.sqrt(p * p + l * l)
    qr = np.sqrt((r + p) / 2.0)
    qi = l / (2.0 * qr)
    w = np.exp(-(qr + 1j * qi))
    g = b / (2.0 * r) * (qr - 1j * qi)

    def pack(t):
        t = t.reshape(2, H, N)
        return np.stack([t.real, t.imag], axis=1).astype(np.float32)

    source = np.stack([pack(np.conj(g * w ** (NZ - 1 - s))) for s in range(NZ)])
    return np.stack([pack(w), pack(g)]), source


def split(a):
    hi = a.astype(jnp.bfloat16)
    lo = (a - hi.astype(jnp.float32)).astype(jnp.bfloat16)
    return hi, lo


def dot_right(a, m_ref, q):
    hi, lo = split(a)
    mh, ml = m_ref[q, 0], m_ref[q, 1]
    return jnp.dot(
        jnp.concatenate([hi, lo, hi], axis=1),
        jnp.concatenate([mh, mh, ml], axis=0),
        preferred_element_type=jnp.float32,
    )


def dot_left(m_ref, q, a):
    hi, lo = split(a)
    mh, ml = m_ref[q, 0], m_ref[q, 1]
    return jnp.dot(
        jnp.concatenate([mh, mh, ml], axis=1),
        jnp.concatenate([hi, lo, hi], axis=0),
        preferred_element_type=jnp.float32,
    )


def forward_plane(re, im, right, left, store):
    halves = []
    for q in (0, 1):
        if q == 0:
            a = jnp.concatenate([re[:, :H] + re[:, H:], im[:, :H] + im[:, H:]], axis=1)
        else:
            a = jnp.concatenate([re[:, :H] - re[:, H:], im[:, :H] - im[:, H:]], axis=1)
        halves.append(dot_right(a, right, q))
    for q in (0, 1):
        parts = []
        for t in halves:
            u = t[:H] + t[H:] if q == 0 else t[:H] - t[H:]
            parts.append(jnp.concatenate([u[:, :H], u[:, H:]], axis=0))
        store(q, dot_left(left, q, jnp.concatenate(parts, axis=1)))


def inverse_plane(load, right, left):
    e = [dot_left(right, q, load(q)) for q in (0, 1)]
    e = [part * (1.0 / (N * N)) for part in e]
    top, bottom = e[0] + e[1], e[0] - e[1]
    re = jnp.concatenate([top[:H], bottom[:H]], axis=0)
    im = jnp.concatenate([top[H:], bottom[H:]], axis=0)
    e = []
    for q in (0, 1):
        z = jnp.concatenate([re[:, q * H : (q + 1) * H], im[:, q * H : (q + 1) * H]], axis=1)
        e.append(dot_right(z, left, q))
    low, high = e[0] + e[1], e[0] - e[1]
    re = jnp.concatenate([low[:, :H], high[:, :H]], axis=1)
    im = jnp.concatenate([low[:, H:], high[:, H:]], axis=1)
    return re, im


def cmul(a, b):
    return a[0] * b[0] - a[1] * b[1], a[0] * b[1] + a[1] * b[0]


def cadd(a, b):
    return a[0] + b[0], a[1] + b[1]


def csub(a, b):
    return a[0] - b[0], a[1] - b[1]


def tile_sum(a):
    a = a[:, :H] + a[:, H:]
    if a.shape[0] > 8:
        a = jnp.sum(a.reshape(a.shape[0] // 8, 8, H), axis=0)
    return a


def total_of(tile):
    return jnp.sum(jnp.sum(tile, axis=0, keepdims=True), axis=1, keepdims=True)


def kernel(
    angles, block, meas, right, left, wg, source_table,
    fields, descent, misfit,
    plane, c4, s_buf, f_buf, w_buf, gh0, gh1, g0, g1, r_buf, ybuf, red_out, red_in,
    mh, h7, part, rs_in, ar_out, ar1, ar2,
    ga_s, ga_r, gb_s, gb_r, x_s, x_r, rd_s, rd_r, pg_s, pg_r, ht_s, ht_r, h7_sem,
    rs_s, rs_r, a1_s, a1_r, a2_s, a2_r,
):
    illum = lax.axis_index("illum")
    slab = lax.axis_index("slab")
    chip = slab // 2
    core = slab - 2 * chip
    other = (illum, slab + 1 - 2 * core)

    def illum_peer(k):
        return (lax.rem(illum + k, ILLUMS), slab)

    def slab_peer(k):
        return (illum, lax.rem(slab + k, NZ))

    load_h7 = pltpu.make_async_copy(source_table.at[slab], h7, h7_sem)
    load_h7.start()

    barrier = pltpu.get_barrier_semaphore()
    for k in range(1, ILLUMS):
        pl.semaphore_signal(barrier, inc=1, device_id=illum_peer(k), device_id_type=MESH)
    for k in range(1, NZ):
        pl.semaphore_signal(barrier, inc=1, device_id=slab_peer(k), device_id_type=MESH)
    pl.semaphore_wait(barrier, ILLUMS - 1 + NZ - 1)

    my_rows = pl.ds(pl.multiple_of(illum * 8, 8), 8)
    for k in range(1, ILLUMS):
        pltpu.make_async_remote_copy(
            src_ref=block, dst_ref=plane.at[my_rows], send_sem=ga_s, recv_sem=ga_r,
            device_id=illum_peer(k), device_id_type=MESH,
        ).start()
    plane[my_rows, :] = block[...]

    def angle_row(i):
        return jnp.sin(TILT * jnp.full((1, H), angles[0, i], jnp.int32).astype(jnp.float32))

    sine_x, sine_y = angle_row(0), angle_row(1)
    cos_z = jnp.sqrt(1.0 - sine_x * sine_x - sine_y * sine_y)
    x_at = lax.broadcasted_iota(jnp.int32, (N, H), 0).astype(jnp.float32)
    x_phase = WAVE * (sine_x * x_at)
    ex = jnp.cos(x_phase), jnp.sin(x_phase)
    y_at = lax.broadcasted_iota(jnp.int32, (1, H), 1).astype(jnp.float32)

    def incident(z):
        halves = []
        zf = jnp.full((1, H), z, jnp.int32).astype(jnp.float32)
        for q in (0, 1):
            phase = WAVE * (sine_y * (y_at + float(q * H)) + cos_z * zf)
            halves.append(cmul(ex, (jnp.cos(phase), jnp.sin(phase))))
        return tuple(jnp.concatenate([halves[0][i], halves[1][i]], axis=1) for i in (0, 1))

    def store_to(ref, p):
        def store(q, value):
            ref[p, q, 0] = value[:H]
            ref[p, q, 1] = value[H:]
        return store

    def load_from(ref, p):
        return lambda q: jnp.concatenate([ref[p, q, 0], ref[p, q, 1]], axis=0)

    def store_mh(q, value):
        mh[q, 0] = value[:H]
        mh[q, 1] = value[H:]

    forward_plane(meas[0], meas[1], right, left, store_mh)

    def sent(n, src, dst, s_sem, r_sem, dev):
        return pltpu.make_async_remote_copy(
            src_ref=src, dst_ref=dst, send_sem=s_sem, recv_sem=r_sem, device_id=dev, device_id_type=MESH
        )

    def wait_bytes(ref, sem):
        pltpu.make_async_copy(ref, ref, sem).wait()

    wait_bytes(plane.at[pl.ds(0, (ILLUMS - 1) * 8)], ga_s)
    wait_bytes(plane.at[pl.ds(0, (ILLUMS - 1) * 8)], ga_r)

    high = slab // 4
    slot = slab + high * (7 - 2 * slab)
    for k in range(1, 4):
        dest = 2 * lax.rem(chip + k, 4) + high
        sent(0, plane, c4.at[slot], gb_s.at[k], gb_r.at[slot], (illum, dest)).start()

    @pl.when(core != high)
    def _():
        sent(0, plane, c4.at[slot], gb_s.at[0], gb_r.at[slot], other).start()

    @pl.when(core == high)
    def _():
        c4[slot] = plane[...]

    for k in range(1, 4):
        sent(0, plane, c4.at[slot], gb_s.at[k], gb_r.at[slot], other).wait_send()

    @pl.when(core != high)
    def _():
        sent(0, plane, c4.at[slot], gb_s.at[0], gb_r.at[slot], other).wait_send()

    for k in range(4):
        @pl.when((core != high) | (slot != k))
        def _():
            sent(0, plane, c4.at[k], gb_s.at[0], gb_r.at[k], other).wait_recv()

    def global_z(k):
        return k + core * (7 - 2 * k)

    @pl.loop(0, 4)
    def _(p):
        re, im = incident(global_z(p))
        c = c4[p]
        forward_plane(c * re, c * im, right, left, store_to(s_buf, p))

    def where_q(q):
        return q // 2, (q % 2) * CR

    def exchange(n, q):
        xp, base = where_q(q)
        rows = pl.ds(base, CR)
        return sent(
            0, f_buf.at[2, xp, :, rows], ybuf.at[n, xp, :, rows], x_s.at[n, q], x_r.at[n, q], other
        )

    def pair(ref, *at):
        *lead, rows = at
        return ref[(*lead, 0, rows)], ref[(*lead, 1, rows)]

    def put(ref, value, *at):
        *lead, rows = at
        ref[(*lead, 0, rows)] = value[0]
        ref[(*lead, 1, rows)] = value[1]

    def table(t, xp, rows, sign):
        re, im = pair(wg, t, xp, rows)
        return re, im if sign > 0 else -im

    def forward_chain(values, w, xp, rows):
        f = values[0]
        for k in range(1, 4):
            f = cadd(values[k], cmul(w, f))
            put(f_buf, f, k - 1, xp, rows)

    def first_pass(src, n, sign):
        for q in range(CHUNKS):
            xp, base = where_q(q)

            @pl.loop(0, CR // 8)
            def _(i):
                rows = pl.ds(pl.multiple_of(base + i * 8, 8), 8)
                forward_chain([pair(src, k, xp, rows) for k in range(4)], table(0, xp, rows, sign), xp, rows)

            exchange(n, q).start()

    def second_pass(src, n, sign, emit, acc):
        for q in range(CHUNKS):
            xp, base = where_q(q)
            exchange(n, q).wait()

            def step(i, acc):
                rows = pl.ds(pl.multiple_of(base + i * 8, 8), 8)
                w, g = table(0, xp, rows, sign), table(1, xp, rows, sign)
                t = pair(ybuf, n, xp, rows)
                out = [None] * 4
                for k in (3, 2, 1, 0):
                    u = cmul(w, t)
                    v = pair(src, k, xp, rows)
                    f = v if k == 0 else pair(f_buf, k - 1, xp, rows)
                    out[k] = cmul(g, cadd(f, u))
                    if k:
                        t = cadd(v, u)
                return emit(out, xp, rows, acc)

            acc = lax.fori_loop(0, CR // 8, step, acc)
            if emit.following is not None:
                exchange(emit.following, q).start()
        return acc

    zero = jnp.zeros((8, N), jnp.float32)

    def norm(acc, value):
        return acc + (value[0] * value[0] + value[1] * value[1])

    def reduce_start(n, rows):
        for i, tile in enumerate(rows):
            red_out[n, i] = tile
        copy = sent(0, red_out.at[n], red_in.at[n], rd_s.at[n], rd_r.at[n], other)
        copy.start()
        return copy

    def emit_first(out, xp, rows, acc):
        for k in range(4):
            put(w_buf, out[k], k, xp, rows)
        w = table(0, xp, rows, -1)
        forward_chain(out, w, xp, rows)
        return acc

    emit_first.following = 1

    def emit_back(out, xp, rows, acc):
        for k in range(4):
            put(s_buf, out[k], k, xp, rows)
        return acc

    emit_back.following = None

    first_pass(s_buf, 0, 1)
    second_pass(s_buf, 0, 1, emit_first, 0)

    @pl.loop(0, 4)
    def _(p):
        re, im = inverse_plane(load_from(w_buf, p), right, left)
        r_buf[p, 0] = re
        r_buf[p, 1] = im

    second_pass(w_buf, 1, -1, emit_back, 0)

    def gradient_step(p, acc):
        re, im = inverse_plane(load_from(s_buf, p), right, left)
        c = c4[p]
        re = r_buf[p, 0] - c * re
        im = r_buf[p, 1] - c * im
        g0[p, 0] = re
        g0[p, 1] = im
        acc = acc + tile_sum(re * re + im * im)
        forward_plane(c * re, c * im, right, left, store_to(s_buf, p))
        return acc

    zz0 = lax.fori_loop(0, 4, gradient_step, jnp.zeros((8, H), jnp.float32))

    sender = chip // 2
    send_index = 2 * chip + 1 + sender * (6 - 4 * chip)
    own_index = jnp.where(core == sender, 2 * chip + sender * (6 - 4 * chip), 4)

    def plane_copy(n, ref):
        return sent(0, ref.at[send_index], ref.at[4], pg_s.at[n], pg_r.at[n], other)

    def hat_copy(n, ref):
        return sent(0, ref.at[0], ref.at[4], ht_s.at[n], ht_r.at[n], other)

    first_pass(s_buf, 2, 1)

    @pl.when(core == sender)
    def _():
        plane_copy(0, g0).start()

    @pl.loop(0, 4)
    def _(p):
        forward_plane(g0[p, 0], g0[p, 1], right, left, store_to(gh0, p))

    @pl.when(core == 1)
    def _():
        hat_copy(0, gh0).start()

    def emit_image(out, xp, rows, acc):
        w = table(0, xp, rows, -1)
        image = []
        for k in range(4):
            m = csub(pair(gh0, k, xp, rows), out[k])
            acc = norm(acc, m)
            put(w_buf, m, k, xp, rows)
            image.append(m)
        forward_chain(image, w, xp, rows)
        return acc

    emit_image.following = 3
    mm0 = second_pass(s_buf, 2, 1, emit_image, zero)
    red0 = reduce_start(0, (zz0, tile_sum(mm0)))

    @pl.loop(0, 4)
    def _(p):
        re, im = inverse_plane(load_from(w_buf, p), right, left)
        r_buf[p, 0] = re
        r_buf[p, 1] = im

    second_pass(w_buf, 3, -1, emit_back, 0)
    red0.wait()
    zz_first = total_of(red_out[0, 0] + red_in[0, 0])
    mm_first = total_of(red_out[0, 1] + red_in[0, 1]) * (1.0 / (N * N))
    alpha0 = zz_first / mm_first

    def next_step(p, acc):
        re, im = inverse_plane(load_from(s_buf, p), right, left)
        c = c4[p]
        re = g0[p, 0] - alpha0 * (r_buf[p, 0] - c * re)
        im = g0[p, 1] - alpha0 * (r_buf[p, 1] - c * im)
        g1[p, 0] = re
        g1[p, 1] = im
        acc = acc + tile_sum(re * re + im * im)
        forward_plane(c * re, c * im, right, left, store_to(s_buf, p))
        return acc

    zz1 = lax.fori_loop(0, 4, next_step, jnp.zeros((8, H), jnp.float32))
    red1 = reduce_start(1, (zz1,))
    first_pass(s_buf, 4, 1)

    @pl.when(core == sender)
    def _():
        plane_copy(1, g1).start()

    @pl.loop(0, 4)
    def _(p):
        forward_plane(g1[p, 0], g1[p, 1], right, left, store_to(gh1, p))

    @pl.when(core == 1)
    def _():
        hat_copy(1, gh1).start()

    red1.wait()
    zz_second = total_of(red_out[1, 0] + red_in[1, 0])
    beta0 = zz_second / zz_first

    def emit_last(out, xp, rows, acc):
        for k in range(4):
            m = csub(pair(gh1, k, xp, rows), out[k])
            old = pair(w_buf, k, xp, rows)
            acc = norm(acc, (m[0] + beta0 * old[0], m[1] + beta0 * old[1]))
        return acc

    emit_last.following = None
    mm1 = second_pass(s_buf, 4, 1, emit_last, zero)
    red2 = reduce_start(2, (tile_sum(mm1),))

    @pl.when(core == sender)
    def _():
        plane_copy(0, g0).wait_send()
        plane_copy(1, g1).wait_send()

    @pl.when(core != sender)
    def _():
        plane_copy(0, g0).wait_recv()
        plane_copy(1, g1).wait_recv()

    @pl.when(core == 1)
    def _():
        hat_copy(0, gh0).wait_send()
        hat_copy(1, gh1).wait_send()

    @pl.when(core == 0)
    def _():
        hat_copy(0, gh0).wait_recv()
        hat_copy(1, gh1).wait_recv()

    load_h7.wait()
    inc_re, inc_im = incident(slab)
    red2.wait()
    mm_second = total_of(red_out[2, 0] + red_in[2, 0]) * (1.0 / (N * N))
    alpha1 = zz_second / mm_second
    weight0 = alpha0 + alpha1 * beta0

    hat = 4 * (1 - core)
    for xp in (0, 1):
        s7 = tuple(weight0 * gh0[hat, xp, i] + alpha1 * gh1[hat, xp, i] - mh[xp, i] for i in (0, 1))
        back = cmul((h7[xp, 0], h7[xp, 1]), s7)
        w_buf[0, xp, 0] = back[0]
        w_buf[0, xp, 1] = back[1]
    back_re, back_im = inverse_plane(load_from(w_buf, 0), right, left)
    more_re = weight0 * g0[own_index, 0] + alpha1 * g1[own_index, 0]
    more_im = weight0 * g0[own_index, 1] + alpha1 * g1[own_index, 1]
    sol_re = inc_re + more_re
    sol_im = inc_im + more_im
    fields[0] = sol_re
    fields[1] = sol_im
    part[...] = sol_re * back_re + sol_im * back_im

    for k in range(1, ILLUMS):
        peer = illum_peer(k)
        rows = pl.ds(pl.multiple_of(peer[0] * 8, 8), 8)
        sent(0, part.at[rows], rs_in.at[illum], rs_s, rs_r, peer).start()
    rs_in[illum] = part[my_rows, :]
    miss_re = more_re - meas[0]
    miss_im = more_im - meas[1]
    misfit_tile = tile_sum(miss_re * miss_re + miss_im * miss_im)
    is_last = jnp.where(slab == NZ - 1, 0.5, 0.0)
    misfit_row = is_last * jnp.sum(misfit_tile, axis=0, keepdims=True)
    wait_bytes(rs_in.at[pl.ds(0, ILLUMS - 1)], rs_s)
    wait_bytes(rs_in.at[pl.ds(0, ILLUMS - 1)], rs_r)

    rows = jnp.sum(rs_in[...], axis=0)
    square_row = jnp.sum(tile_sum(rows * rows), axis=0, keepdims=True)
    at = lax.broadcasted_iota(jnp.int32, (8, H), 0)
    ar_out[0] = jnp.where(at == 0, square_row, jnp.where(at == 1, misfit_row, 0.0))
    for k in range(1, NZ):
        sent(0, ar_out.at[0], ar1.at[slab], a1_s, a1_r, slab_peer(k)).start()
    ar1[slab] = ar_out[0]
    wait_bytes(ar1.at[pl.ds(0, NZ - 1)], a1_s)
    wait_bytes(ar1.at[pl.ds(0, NZ - 1)], a1_r)
    ar_out[1] = jnp.sum(ar1[...], axis=0)
    for k in range(1, ILLUMS):
        sent(0, ar_out.at[1], ar2.at[illum], a2_s, a2_r, illum_peer(k)).start()
    ar2[illum] = ar_out[1]
    wait_bytes(ar2.at[pl.ds(0, ILLUMS - 1)], a2_s)
    wait_bytes(ar2.at[pl.ds(0, ILLUMS - 1)], a2_r)
    sums = jnp.sum(ar2[...], axis=0)
    square = jnp.sum(sums[0:1], axis=1, keepdims=True)
    descent[...] = rows / jnp.sqrt(square * (1.0 / (NZ * N * N)) + 1e-06)
    misfit[0, 0] = jnp.sum(sums[1:2])


def body(angles, contrast, measured):
    right, left = dft_tables()
    wg, source = depth_tables()
    vmem = pl.BlockSpec(memory_space=pltpu.VMEM)
    smem = pl.BlockSpec(memory_space=pltpu.SMEM)
    anyspace = pl.BlockSpec(memory_space=pl.ANY)
    f32 = jnp.float32
    dma = pltpu.SemaphoreType.DMA
    spectral = (2, 2, H, N)
    fields, descent, misfit = pl.pallas_call(
        kernel,
        out_shape=(
            jax.ShapeDtypeStruct((2, N, N), f32),
            jax.ShapeDtypeStruct((8, N), f32),
            jax.ShapeDtypeStruct((1, 1), f32),
        ),
        in_specs=[smem, vmem, vmem, vmem, vmem, vmem, anyspace],
        out_specs=(vmem, vmem, smem),
        scratch_shapes=[
            pltpu.VMEM((N, N), f32),
            pltpu.VMEM((4, N, N), f32),
            pltpu.VMEM((4, *spectral), f32),
            pltpu.VMEM((3, *spectral), f32),
            pltpu.VMEM((4, *spectral), f32),
            pltpu.VMEM((5, *spectral), f32),
            pltpu.VMEM((5, *spectral), f32),
            pltpu.VMEM((5, 2, N, N), f32),
            pltpu.VMEM((5, 2, N, N), f32),
            pltpu.VMEM((4, 2, N, N), f32),
            pltpu.VMEM((5, *spectral), f32),
            pltpu.VMEM((3, 2, 8, H), f32),
            pltpu.VMEM((3, 2, 8, H), f32),
            pltpu.VMEM(spectral, f32),
            pltpu.VMEM(spectral, f32),
            pltpu.VMEM((N, N), f32),
            pltpu.VMEM((ILLUMS, 8, N), f32),
            pltpu.VMEM((2, 8, H), f32),
            pltpu.VMEM((NZ, 8, H), f32),
            pltpu.VMEM((ILLUMS, 8, H), f32),
            dma, dma, dma((4,)), dma((4,)),
            dma((5, CHUNKS)), dma((5, CHUNKS)),
            dma((3,)), dma((3,)), dma((2,)), dma((2,)), dma((2,)), dma((2,)), dma,
            dma, dma, dma, dma, dma, dma,
        ],
        compiler_params=pltpu.CompilerParams(
            collective_id=0, has_side_effects=True, vmem_limit_bytes=48 * 1024 * 1024
        ),
    )(
        angles, contrast.reshape(8, N), measured.reshape(2, N, N),
        jnp.asarray(right), jnp.asarray(left), jnp.asarray(wg), jnp.asarray(source),
    )
    return fields.reshape(1, 2, 1, N, N), descent.reshape(1, 8, N), misfit.reshape(())


def solution(mesh):
    return jax.shard_map(
        body,
        mesh=mesh,
        in_specs=(P("illum", None), P("slab", "illum", None), P("illum", None, None, None)),
        out_specs=(P("illum", None, "slab", None, None), P("slab", "illum", None), P()),
        check_vma=False,
    )
```

```python
import functools
import math

import jax
import jax.numpy as jnp
import numpy as np
from jax import lax
from jax.experimental import pallas as pl
from jax.experimental.pallas import tpu as pltpu
from jax.sharding import PartitionSpec as P

MESH = pl.DeviceIdType.MESH
N = 256
H = 128
NZ = 8
ILLUMS = 32
WAVE = 2.0 * math.pi / 8.0
DAMPING = 0.2
TILT = 0.04
CHUNKS = 4
CR = 64


def far_first(a, b):
    def length(step):
        return min(step[0], a - step[0]) + min(step[1], b - step[1])

    steps = [(i, j) for i in range(a) for j in range(b) if i or j]
    return sorted(steps, key=length, reverse=True)


ILLUM_STEPS = far_first(4, 8)
CHIP_STEPS = far_first(4, 4)
DEPTH_STEPS = sorted(range(1, 8), key=lambda k: -min(k, 8 - k))


def dft_tables():
    n = np.arange(H)[:, None]
    m = np.arange(H)[None, :]
    out = []
    for q in (0, 1):
        theta = -2.0 * np.pi / N * ((n * (2 * m + q)) % N)
        c, s = np.cos(theta), np.sin(theta)
        out.append(np.block([[c, s], [-s, c]]))
    return np.stack(out + [r.T for r in out]).astype(np.float32)


def depth_tables():
    order = np.concatenate([np.arange(0, N, 2), np.arange(1, N, 2)])
    sym = 2.0 - 2.0 * np.cos(2.0 * np.pi / N * order)
    b = WAVE * WAVE
    p = sym[:, None] + sym[None, :] - b
    l = b * DAMPING
    r = np.sqrt(p * p + l * l)
    qr = np.sqrt((r + p) / 2.0)
    qi = l / (2.0 * qr)
    w = np.exp(-(qr + 1j * qi))
    g = b / (2.0 * r) * (qr - 1j * qi)

    def pack(t):
        t = t.reshape(2, H, N)
        return np.stack([t.real, t.imag], axis=1).astype(np.float32)

    source = np.stack([pack(np.conj(g * w ** (NZ - 1 - s))) for s in range(NZ)])
    return np.stack([pack(w), pack(g)]), source


def split(a):
    hi = a.astype(jnp.bfloat16)
    lo = (a - hi.astype(jnp.float32)).astype(jnp.bfloat16)
    return hi, lo


def dot_right(a, m_ref, q):
    hi, lo = split(a)
    mh, ml = m_ref[q, 0], m_ref[q, 1]
    return jnp.dot(
        jnp.concatenate([hi, lo, hi], axis=1),
        jnp.concatenate([mh, mh, ml], axis=0),
        preferred_element_type=jnp.float32,
    )


def dot_left(m_ref, q, a):
    hi, lo = split(a)
    mh, ml = m_ref[q, 0], m_ref[q, 1]
    return jnp.dot(
        jnp.concatenate([mh, mh, ml], axis=1),
        jnp.concatenate([hi, lo, hi], axis=0),
        preferred_element_type=jnp.float32,
    )


def forward_plane(re, im, right, left, store):
    halves = []
    for q in (0, 1):
        if q == 0:
            a = jnp.concatenate([re[:, :H] + re[:, H:], im[:, :H] + im[:, H:]], axis=1)
        else:
            a = jnp.concatenate([re[:, :H] - re[:, H:], im[:, :H] - im[:, H:]], axis=1)
        halves.append(dot_right(a, right, q))
    for q in (0, 1):
        parts = []
        for t in halves:
            u = t[:H] + t[H:] if q == 0 else t[:H] - t[H:]
            parts.append(jnp.concatenate([u[:, :H], u[:, H:]], axis=0))
        store(q, dot_left(left, q, jnp.concatenate(parts, axis=1)))


def inverse_plane(load, right, left):
    e = [dot_left(right, q, load(q)) for q in (0, 1)]
    e = [part * (1.0 / (N * N)) for part in e]
    top, bottom = e[0] + e[1], e[0] - e[1]
    re = jnp.concatenate([top[:H], bottom[:H]], axis=0)
    im = jnp.concatenate([top[H:], bottom[H:]], axis=0)
    e = []
    for q in (0, 1):
        z = jnp.concatenate([re[:, q * H : (q + 1) * H], im[:, q * H : (q + 1) * H]], axis=1)
        e.append(dot_right(z, left, q))
    low, high = e[0] + e[1], e[0] - e[1]
    re = jnp.concatenate([low[:, :H], high[:, :H]], axis=1)
    im = jnp.concatenate([low[:, H:], high[:, H:]], axis=1)
    return re, im


def cmul(a, b):
    return a[0] * b[0] - a[1] * b[1], a[0] * b[1] + a[1] * b[0]


def cadd(a, b):
    return a[0] + b[0], a[1] + b[1]


def csub(a, b):
    return a[0] - b[0], a[1] - b[1]


def tile_sum(a):
    a = a[:, :H] + a[:, H:]
    if a.shape[0] > 8:
        a = jnp.sum(a.reshape(a.shape[0] // 8, 8, H), axis=0)
    return a


def total_of(tile):
    return jnp.sum(jnp.sum(tile, axis=0, keepdims=True), axis=1, keepdims=True)


def kernel(
    angles_in, block, meas_in, dft_in, wg_in, source_table,
    fields, descent, misfit,
    angles, meas, dft, right, left, wg, inc, zbuf, c4, s_buf, f_buf, w_buf, gh0, gh1, g0, g1, r_buf, ybuf, red_out, red_in,
    mh, h7, part, rs_in, ar_out, ar1, ar2,
    in_sem, ga_s, ga_r, gb_s, go_s, gb_r, x_s, x_r, rd_s, rd_r, pg_s, pg_r, ht_s, ht_r,
    rs_s, rs_r, a1_s, a1_r, a2_s, a2_r,
):
    illum = lax.axis_index("illum")
    slab = lax.axis_index("slab")
    chip = slab // 2
    core = slab - 2 * chip
    other = (illum, slab + 1 - 2 * core)

    x, z = illum // 8, lax.rem(illum, 8)

    def illum_at(dx, dz):
        return lax.rem(x + dx, 4) * 8 + lax.rem(z + dz, 8)

    def slab_peer(k):
        return (illum, lax.rem(slab + k, NZ))

    def sent(src, dst, s_sem, r_sem, dev):
        return pltpu.make_async_remote_copy(
            src_ref=src, dst_ref=dst, send_sem=s_sem, recv_sem=r_sem, device_id=dev, device_id_type=MESH
        )

    def wait_bytes(ref, sem):
        pltpu.make_async_copy(ref, ref, sem).wait()

    barrier = pltpu.get_barrier_semaphore()

    def greet(peer):
        pl.semaphore_signal(barrier, inc=1, device_id=peer, device_id_type=MESH)

    for dx, dz in ILLUM_STEPS:
        greet((illum_at(dx, dz), slab))
    for dx in (2, 1, 3):
        for k in range(4):
            greet((illum_at(dx, 0), 4 * core + k))
    for k in range(1, NZ):
        greet(slab_peer(k))

    z_rows = pl.ds(pl.multiple_of(z * 8, 8), 8)
    loads = [
        pltpu.make_async_copy(src, dst, in_sem.at[i])
        for i, (src, dst) in enumerate((
            (block, zbuf.at[z_rows]), (angles_in, angles), (meas_in, meas), (dft_in, dft),
            (wg_in, wg), (source_table.at[slab], h7),
        ))
    ]
    for load in loads:
        load.start()
    for load in loads[:4]:
        load.wait()
    for q in (0, 1):
        for i, value in enumerate(split(dft[q])):
            right[q, i] = value
        for i, value in enumerate(split(dft[2 + q])):
            left[q, i] = value

    def store_mh(q, value):
        mh[q, 0] = value[:H]
        mh[q, 1] = value[H:]

    forward_plane(meas[0], meas[1], right, left, store_mh)
    pl.semaphore_wait(barrier, ILLUMS - 1 + NZ - 1 + 12)

    for dz in DEPTH_STEPS:
        sent(zbuf.at[z_rows], zbuf.at[z_rows], ga_s, ga_r, (illum_at(0, dz), slab)).start()

    def angle_row(i):
        return jnp.sin(TILT * jnp.full((1, H), angles[0, i], jnp.int32).astype(jnp.float32))

    sine_x, sine_y = angle_row(0), angle_row(1)
    cos_z = jnp.sqrt(1.0 - sine_x * sine_x - sine_y * sine_y)
    x_at = lax.broadcasted_iota(jnp.int32, (N, H), 0).astype(jnp.float32)
    x_phase = WAVE * (sine_x * x_at)
    ex = jnp.cos(x_phase), jnp.sin(x_phase)
    y_at = lax.broadcasted_iota(jnp.int32, (1, H), 1).astype(jnp.float32)

    def incident(z):
        halves = []
        zf = jnp.full((1, H), z, jnp.int32).astype(jnp.float32)
        for q in (0, 1):
            phase = WAVE * (sine_y * (y_at + float(q * H)) + cos_z * zf)
            halves.append(cmul(ex, (jnp.cos(phase), jnp.sin(phase))))
        return tuple(jnp.concatenate([halves[0][i], halves[1][i]], axis=1) for i in (0, 1))

    def store_to(ref, p):
        def store(q, value):
            ref[p, q, 0] = value[:H]
            ref[p, q, 1] = value[H:]
        return store

    def load_from(ref, p):
        return lambda q: jnp.concatenate([ref[p, q, 0], ref[p, q, 1]], axis=0)

    def global_z(k):
        return k + core * (7 - 2 * k)

    def keep_incident(p):
        inc[p, 0], inc[p, 1] = incident(global_z(p))

    pl.loop(0, 4)(keep_incident)

    wait_bytes(zbuf.at[pl.ds(0, 56)], ga_s)
    wait_bytes(zbuf.at[pl.ds(0, 56)], ga_r)

    high = slab // 4
    slot = slab + high * (7 - 2 * slab)
    x_rows = pl.ds(pl.multiple_of(x * 64, 64), 64)
    for dx, dy in CHIP_STEPS:
        dest = 2 * lax.rem(chip + dy, 4) + high
        sent(zbuf, c4.at[slot, x_rows], gb_s, gb_r.at[slot], (illum_at(dx, 0), dest)).start()

    def to_other():
        return sent(zbuf, c4.at[slot, x_rows], go_s, gb_r.at[slot], other)

    @pl.when(core != high)
    def _():
        to_other().start()

    @pl.when(core == high)
    def _():
        c4[slot, x_rows] = zbuf[...]

    def wait_plane(k):
        here = (core == high) & (slot == k)

        @pl.when(here)
        def _():
            wait_bytes(c4.at[k, pl.ds(0, 192)], gb_r.at[k])

        @pl.when(jnp.logical_not(here))
        def _():
            wait_bytes(c4.at[k], gb_r.at[k])

    for first in (0, 2):
        wait_plane(first)
        wait_plane(first + 1)
        for p in (first, first + 1):
            c = c4[p]
            forward_plane(c * inc[p, 0], c * inc[p, 1], right, left, store_to(s_buf, p))

    @pl.when(core != high)
    def _():
        to_other().wait_send()

    for _ in range(15):
        wait_bytes(zbuf, gb_s)
    loads[4].wait()

    def where_q(q):
        return q // 2, (q % 2) * CR

    def exchange(n, q):
        xp, base = where_q(q)
        rows = pl.ds(base, CR)
        return sent(
            f_buf.at[2, xp, :, rows], ybuf.at[n, xp, :, rows], x_s.at[n, q], x_r.at[n, q], other
        )

    def pair(ref, *at):
        *lead, rows = at
        return ref[(*lead, 0, rows)], ref[(*lead, 1, rows)]

    def put(ref, value, *at):
        *lead, rows = at
        ref[(*lead, 0, rows)] = value[0]
        ref[(*lead, 1, rows)] = value[1]

    def table(t, xp, rows, sign):
        re, im = pair(wg, t, xp, rows)
        return re, im if sign > 0 else -im

    def forward_chain(values, w, xp, rows):
        f = values[0]
        for k in range(1, 4):
            f = cadd(values[k], cmul(w, f))
            put(f_buf, f, k - 1, xp, rows)

    def first_pass(src, n, sign):
        for q in range(CHUNKS):
            xp, base = where_q(q)

            @pl.loop(0, CR // 8)
            def _(i):
                rows = pl.ds(pl.multiple_of(base + i * 8, 8), 8)
                forward_chain([pair(src, k, xp, rows) for k in range(4)], table(0, xp, rows, sign), xp, rows)

            exchange(n, q).start()

    def second_pass(src, n, sign, emit, acc):
        for q in range(CHUNKS):
            xp, base = where_q(q)
            exchange(n, q).wait()

            def step(i, acc):
                rows = pl.ds(pl.multiple_of(base + i * 8, 8), 8)
                w, g = table(0, xp, rows, sign), table(1, xp, rows, sign)
                t = pair(ybuf, n, xp, rows)
                out = [None] * 4
                for k in (3, 2, 1, 0):
                    u = cmul(w, t)
                    v = pair(src, k, xp, rows)
                    f = v if k == 0 else pair(f_buf, k - 1, xp, rows)
                    out[k] = cmul(g, cadd(f, u))
                    if k:
                        t = cadd(v, u)
                return emit(out, xp, rows, acc)

            acc = lax.fori_loop(0, CR // 8, step, acc)
            if emit.following is not None:
                exchange(emit.following, q).start()
        return acc

    zero = jnp.zeros((8, N), jnp.float32)

    def norm(acc, value):
        return acc + (value[0] * value[0] + value[1] * value[1])

    def reduce_start(n, rows):
        for i, tile in enumerate(rows):
            red_out[n, i] = tile
        used = pl.ds(0, len(rows))
        copy = sent(red_out.at[n, used], red_in.at[n, used], rd_s.at[n], rd_r.at[n], other)
        copy.start()
        return copy

    def emit_first(out, xp, rows, acc):
        for k in range(4):
            put(w_buf, out[k], k, xp, rows)
        w = table(0, xp, rows, -1)
        forward_chain(out, w, xp, rows)
        return acc

    emit_first.following = 1

    def emit_back(out, xp, rows, acc):
        for k in range(4):
            put(s_buf, out[k], k, xp, rows)
        return acc

    emit_back.following = None

    first_pass(s_buf, 0, 1)
    second_pass(s_buf, 0, 1, emit_first, 0)

    for p in range(4):
        re, im = inverse_plane(load_from(w_buf, p), right, left)
        r_buf[p, 0] = re
        r_buf[p, 1] = im

    second_pass(w_buf, 1, -1, emit_back, 0)

    def gradient_step(p, acc):
        re, im = inverse_plane(load_from(s_buf, p), right, left)
        c = c4[p]
        re = r_buf[p, 0] - c * re
        im = r_buf[p, 1] - c * im
        g0[p, 0] = re
        g0[p, 1] = im
        acc = acc + tile_sum(re * re + im * im)
        forward_plane(c * re, c * im, right, left, store_to(s_buf, p))
        return acc

    zz0 = jnp.zeros((8, H), jnp.float32)
    for p in range(4):
        zz0 = gradient_step(p, zz0)

    sender = chip // 2
    send_index = 2 * chip + 1 + sender * (6 - 4 * chip)
    own_index = jnp.where(core == sender, 2 * chip + sender * (6 - 4 * chip), 4)

    def plane_copy(n, ref):
        return sent(ref.at[send_index], ref.at[4], pg_s.at[n], pg_r.at[n], other)

    def hat_copy(n, ref):
        return sent(ref.at[0], ref.at[4], ht_s.at[n], ht_r.at[n], other)

    first_pass(s_buf, 2, 1)

    @pl.when(core == sender)
    def _():
        plane_copy(0, g0).start()

    for p in range(4):
        forward_plane(g0[p, 0], g0[p, 1], right, left, store_to(gh0, p))

    @pl.when(core == 1)
    def _():
        hat_copy(0, gh0).start()

    def emit_image(out, xp, rows, acc):
        w = table(0, xp, rows, -1)
        image = []
        for k in range(4):
            m = csub(pair(gh0, k, xp, rows), out[k])
            acc = norm(acc, m)
            put(w_buf, m, k, xp, rows)
            image.append(m)
        forward_chain(image, w, xp, rows)
        return acc

    emit_image.following = 3
    mm0 = second_pass(s_buf, 2, 1, emit_image, zero)
    red0 = reduce_start(0, (zz0, tile_sum(mm0)))

    for p in range(4):
        re, im = inverse_plane(load_from(w_buf, p), right, left)
        r_buf[p, 0] = re
        r_buf[p, 1] = im

    second_pass(w_buf, 3, -1, emit_back, 0)
    red0.wait()
    zz_first = total_of(red_out[0, 0] + red_in[0, 0])
    mm_first = total_of(red_out[0, 1] + red_in[0, 1]) * (1.0 / (N * N))
    alpha0 = zz_first / mm_first

    def next_step(p, acc):
        re, im = inverse_plane(load_from(s_buf, p), right, left)
        c = c4[p]
        re = g0[p, 0] - alpha0 * (r_buf[p, 0] - c * re)
        im = g0[p, 1] - alpha0 * (r_buf[p, 1] - c * im)
        g1[p, 0] = re
        g1[p, 1] = im
        acc = acc + tile_sum(re * re + im * im)
        forward_plane(c * re, c * im, right, left, store_to(s_buf, p))
        return acc

    zz1 = jnp.zeros((8, H), jnp.float32)
    for p in range(4):
        zz1 = next_step(p, zz1)
    red1 = reduce_start(1, (zz1,))
    first_pass(s_buf, 4, 1)

    @pl.when(core == sender)
    def _():
        plane_copy(1, g1).start()

    for p in range(4):
        forward_plane(g1[p, 0], g1[p, 1], right, left, store_to(gh1, p))

    @pl.when(core == 1)
    def _():
        hat_copy(1, gh1).start()

    red1.wait()
    zz_second = total_of(red_out[1, 0] + red_in[1, 0])
    beta0 = zz_second / zz_first

    def emit_last(out, xp, rows, acc):
        for k in range(4):
            m = csub(pair(gh1, k, xp, rows), out[k])
            old = pair(w_buf, k, xp, rows)
            acc = norm(acc, (m[0] + beta0 * old[0], m[1] + beta0 * old[1]))
        return acc

    emit_last.following = None
    mm1 = second_pass(s_buf, 4, 1, emit_last, zero)
    red2 = reduce_start(2, (tile_sum(mm1),))

    @pl.when(core == sender)
    def _():
        plane_copy(0, g0).wait_send()
        plane_copy(1, g1).wait_send()

    @pl.when(core != sender)
    def _():
        plane_copy(0, g0).wait_recv()
        plane_copy(1, g1).wait_recv()

    @pl.when(core == 1)
    def _():
        hat_copy(0, gh0).wait_send()
        hat_copy(1, gh1).wait_send()

    @pl.when(core == 0)
    def _():
        hat_copy(0, gh0).wait_recv()
        hat_copy(1, gh1).wait_recv()

    loads[5].wait()
    inc_re, inc_im = incident(slab)
    red2.wait()
    mm_second = total_of(red_out[2, 0] + red_in[2, 0]) * (1.0 / (N * N))
    alpha1 = zz_second / mm_second
    weight0 = alpha0 + alpha1 * beta0

    hat = 4 * (1 - core)
    for xp in (0, 1):
        s7 = tuple(weight0 * gh0[hat, xp, i] + alpha1 * gh1[hat, xp, i] - mh[xp, i] for i in (0, 1))
        back = cmul((h7[xp, 0], h7[xp, 1]), s7)
        w_buf[0, xp, 0] = back[0]
        w_buf[0, xp, 1] = back[1]
    back_re, back_im = inverse_plane(load_from(w_buf, 0), right, left)
    more_re = weight0 * g0[own_index, 0] + alpha1 * g1[own_index, 0]
    more_im = weight0 * g0[own_index, 1] + alpha1 * g1[own_index, 1]
    sol_re = inc_re + more_re
    sol_im = inc_im + more_im
    fields[0] = sol_re
    fields[1] = sol_im
    part[...] = sol_re * back_re + sol_im * back_im

    for dx, dz in ILLUM_STEPS:
        peer = illum_at(dx, dz)
        rows = pl.ds(pl.multiple_of(peer * 8, 8), 8)
        sent(part.at[rows], rs_in.at[illum], rs_s, rs_r, (peer, slab)).start()
    rs_in[illum] = part[pl.ds(pl.multiple_of(illum * 8, 8), 8), :]
    miss_re = more_re - meas[0]
    miss_im = more_im - meas[1]
    misfit_tile = tile_sum(miss_re * miss_re + miss_im * miss_im)
    is_last = jnp.where(slab == NZ - 1, 0.5, 0.0)
    misfit_row = is_last * jnp.sum(misfit_tile, axis=0, keepdims=True)
    wait_bytes(rs_in.at[pl.ds(0, ILLUMS - 1)], rs_s)
    wait_bytes(rs_in.at[pl.ds(0, ILLUMS - 1)], rs_r)

    rows = jnp.sum(rs_in[...], axis=0)
    square_row = jnp.sum(tile_sum(rows * rows), axis=0, keepdims=True)
    at = lax.broadcasted_iota(jnp.int32, (8, H), 0)
    ar_out[0] = jnp.where(at == 0, square_row, jnp.where(at == 1, misfit_row, 0.0))
    for k in range(1, NZ):
        sent(ar_out.at[0], ar1.at[slab], a1_s, a1_r, slab_peer(k)).start()
    ar1[slab] = ar_out[0]
    wait_bytes(ar1.at[pl.ds(0, NZ - 1)], a1_s)
    wait_bytes(ar1.at[pl.ds(0, NZ - 1)], a1_r)
    ar_out[1] = jnp.sum(ar1[...], axis=0)
    for dx, dz in ILLUM_STEPS:
        sent(ar_out.at[1], ar2.at[illum], a2_s, a2_r, (illum_at(dx, dz), slab)).start()
    ar2[illum] = ar_out[1]
    wait_bytes(ar2.at[pl.ds(0, ILLUMS - 1)], a2_s)
    wait_bytes(ar2.at[pl.ds(0, ILLUMS - 1)], a2_r)
    sums = jnp.sum(ar2[...], axis=0)
    square = jnp.sum(sums[0:1], axis=1, keepdims=True)
    descent[...] = rows / jnp.sqrt(square * (1.0 / (NZ * N * N)) + 1e-06)
    misfit[0, 0] = jnp.sum(sums[1:2])


def body(angles, contrast, measured):
    dft = dft_tables()
    wg, source = depth_tables()
    vmem = pl.BlockSpec(memory_space=pltpu.VMEM)
    smem = pl.BlockSpec(memory_space=pltpu.SMEM)
    hbm = pl.BlockSpec(memory_space=pltpu.HBM)
    f32 = jnp.float32
    dma = pltpu.SemaphoreType.DMA
    spectral = (2, 2, H, N)
    fields, descent, misfit = pl.pallas_call(
        kernel,
        out_shape=(
            jax.ShapeDtypeStruct((2, N, N), f32),
            jax.ShapeDtypeStruct((8, N), f32),
            jax.ShapeDtypeStruct((1, 1), f32),
        ),
        in_specs=[hbm] * 6,
        out_specs=(vmem, vmem, smem),
        scratch_shapes=[
            pltpu.SMEM((1, 2), jnp.int32),
            pltpu.VMEM((2, N, N), f32),
            pltpu.VMEM((4, N, N), f32),
            pltpu.VMEM((2, 2, N, N), jnp.bfloat16),
            pltpu.VMEM((2, 2, N, N), jnp.bfloat16),
            pltpu.VMEM((2, *spectral), f32),
            pltpu.VMEM((4, 2, N, N), f32),
            pltpu.VMEM((64, N), f32),
            pltpu.VMEM((4, N, N), f32),
            pltpu.VMEM((4, *spectral), f32),
            pltpu.VMEM((3, *spectral), f32),
            pltpu.VMEM((4, *spectral), f32),
            pltpu.VMEM((5, *spectral), f32),
            pltpu.VMEM((5, *spectral), f32),
            pltpu.VMEM((5, 2, N, N), f32),
            pltpu.VMEM((5, 2, N, N), f32),
            pltpu.VMEM((4, 2, N, N), f32),
            pltpu.VMEM((5, *spectral), f32),
            pltpu.VMEM((3, 2, 8, H), f32),
            pltpu.VMEM((3, 2, 8, H), f32),
            pltpu.VMEM(spectral, f32),
            pltpu.VMEM(spectral, f32),
            pltpu.VMEM((N, N), f32),
            pltpu.VMEM((ILLUMS, 8, N), f32),
            pltpu.VMEM((2, 8, H), f32),
            pltpu.VMEM((NZ, 8, H), f32),
            pltpu.VMEM((ILLUMS, 8, H), f32),
            dma((6,)), dma, dma, dma, dma, dma((4,)),
            dma((5, CHUNKS)), dma((5, CHUNKS)),
            dma((3,)), dma((3,)), dma((2,)), dma((2,)), dma((2,)), dma((2,)),
            dma, dma, dma, dma, dma, dma,
        ],
        compiler_params=pltpu.CompilerParams(
            collective_id=0, has_side_effects=True, vmem_limit_bytes=53 * 1024 * 1024,
        ),
    )(
        angles, contrast.reshape(8, N), measured.reshape(2, N, N),
        jnp.asarray(dft), jnp.asarray(wg), jnp.asarray(source),
    )
    return fields.reshape(1, 2, 1, N, N), descent.reshape(1, 8, N), misfit.reshape(())


def solution(mesh):
    return jax.shard_map(
        body,
        mesh=mesh,
        in_specs=(P("illum", None), P("slab", "illum", None), P("illum", None, None, None)),
        out_specs=(P("illum", None, "slab", None, None), P("slab", "illum", None), P()),
        check_vma=False,
    )
```

```python
import itertools
import math

import jax
import jax.numpy as jnp
import numpy as np
from jax import lax
from jax.experimental import pallas as pl
from jax.experimental.pallas import tpu as pltpu
from jax.sharding import PartitionSpec as P

MESH = pl.DeviceIdType.MESH
N = 256
H = 128
NZ = 8
ILLUMS = 32
WAVE = 2.0 * math.pi / 8.0
DAMPING = 0.2
TILT = 0.04


def far_first(*sizes):
    def length(step):
        return sum(min(k, n - k) for k, n in zip(step, sizes))

    steps = [step for step in itertools.product(*map(range, sizes)) if any(step)]
    return sorted(steps, key=length, reverse=True)


ILLUM_STEPS = far_first(4, 8)
CHIP_STEPS = [(dx, dy) for dy in (2, 0, 1, 3) for dx in (2, 1, 3, 0) if dx or dy]
ALL_STEPS = far_first(4, 8, 4)
CHIPS = 128
DEPTH_STEPS = sorted(range(1, 8), key=lambda k: -min(k, 8 - k))


def dft_tables():
    n = np.arange(H)[:, None]
    m = np.arange(H)[None, :]
    out = []
    for q in (0, 1):
        theta = -2.0 * np.pi / N * ((n * (2 * m + q)) % N)
        c, s = np.cos(theta), np.sin(theta)
        out.append(np.block([[c, s], [-s, c]]))
    return np.stack(out + [r.T for r in out]).astype(np.float32)


def depth_tables():
    order = np.concatenate([np.arange(0, N, 2), np.arange(1, N, 2)])
    sym = 2.0 - 2.0 * np.cos(2.0 * np.pi / N * order)
    b = WAVE * WAVE
    p = sym[:, None] + sym[None, :] - b
    l = b * DAMPING
    r = np.sqrt(p * p + l * l)
    qr = np.sqrt((r + p) / 2.0)
    qi = l / (2.0 * qr)
    w = np.exp(-(qr + 1j * qi))
    g = b / (2.0 * r) * (qr - 1j * qi)

    def pack(t):
        t = t.reshape(2, H, N)
        return np.stack([t.real, t.imag], axis=1).astype(np.float32)

    source = np.stack([pack(np.conj(g * w ** (NZ - 1 - s))) for s in range(NZ)])
    return np.stack([pack(w), pack(g)]), source


def split(a):
    hi = a.astype(jnp.bfloat16)
    lo = (a - hi.astype(jnp.float32)).astype(jnp.bfloat16)
    return hi, lo


def dot_right(a, m_ref, q, exact=True):
    if not exact:
        hi = a.astype(jnp.bfloat16)
        m = jnp.concatenate([m_ref[q, 0], m_ref[q, 1]], axis=0)
        return jnp.dot(jnp.concatenate([hi, hi], axis=1), m, preferred_element_type=jnp.float32)
    hi, lo = split(a)
    mh, ml = m_ref[q, 0], m_ref[q, 1]
    return jnp.dot(
        jnp.concatenate([hi, lo, hi], axis=1),
        jnp.concatenate([mh, mh, ml], axis=0),
        preferred_element_type=jnp.float32,
    )


def dot_left(m_ref, q, a, exact=True):
    if not exact:
        hi = a.astype(jnp.bfloat16)
        m = jnp.concatenate([m_ref[q, 0], m_ref[q, 1]], axis=1)
        return jnp.dot(m, jnp.concatenate([hi, hi], axis=0), preferred_element_type=jnp.float32)
    hi, lo = split(a)
    mh, ml = m_ref[q, 0], m_ref[q, 1]
    return jnp.dot(
        jnp.concatenate([mh, mh, ml], axis=1),
        jnp.concatenate([hi, lo, hi], axis=0),
        preferred_element_type=jnp.float32,
    )


def forward_plane(re, im, right, left, store, exact=True):
    halves = []
    for q in (0, 1):
        if q == 0:
            a = jnp.concatenate([re[:, :H] + re[:, H:], im[:, :H] + im[:, H:]], axis=1)
        else:
            a = jnp.concatenate([re[:, :H] - re[:, H:], im[:, :H] - im[:, H:]], axis=1)
        halves.append(dot_right(a, right, q, exact))
    for q in (0, 1):
        parts = []
        for t in halves:
            u = t[:H] + t[H:] if q == 0 else t[:H] - t[H:]
            parts.append(jnp.concatenate([u[:, :H], u[:, H:]], axis=0))
        store(q, dot_left(left, q, jnp.concatenate(parts, axis=1), exact))


def inverse_plane(load, right, left):
    e = [dot_left(right, q, load(q)) for q in (0, 1)]
    e = [part * (1.0 / (N * N)) for part in e]
    top, bottom = e[0] + e[1], e[0] - e[1]
    re = jnp.concatenate([top[:H], bottom[:H]], axis=0)
    im = jnp.concatenate([top[H:], bottom[H:]], axis=0)
    e = []
    for q in (0, 1):
        z = jnp.concatenate([re[:, q * H : (q + 1) * H], im[:, q * H : (q + 1) * H]], axis=1)
        e.append(dot_right(z, left, q))
    low, high = e[0] + e[1], e[0] - e[1]
    re = jnp.concatenate([low[:, :H], high[:, :H]], axis=1)
    im = jnp.concatenate([low[:, H:], high[:, H:]], axis=1)
    return re, im


def cmul(a, b):
    return a[0] * b[0] - a[1] * b[1], a[0] * b[1] + a[1] * b[0]


def cadd(a, b):
    return a[0] + b[0], a[1] + b[1]


def csub(a, b):
    return a[0] - b[0], a[1] - b[1]


def tile_sum(a):
    a = a[:, :H] + a[:, H:]
    if a.shape[0] > 8:
        a = jnp.sum(a.reshape(a.shape[0] // 8, 8, H), axis=0)
    return a


def total_of(tile):
    return jnp.sum(jnp.sum(tile, axis=0, keepdims=True), axis=1, keepdims=True)


def kernel(
    angles_in, block, meas_in, dft_in, wg_in, source_table,
    fields, descent, misfit,
    angles, meas, dft, right, left, wg, inc, zbuf, c4, s_buf, f_buf, w_buf, gh0, gh1, g0, g1, r_buf, ybuf, red_out, red_in,
    mh, h7, part, rs_in, ar_out, ar_in,
    in_sem, ga_s, ga_r, gb_s, go_s, gb_r, x_s, x_r, rd_s, rd_r, pg_s, pg_r, ht_s, ht_r,
    rs_s, rs_r, a1_s, a1_r, a2_s, a2_r,
):
    illum = lax.axis_index("illum")
    slab = lax.axis_index("slab")
    chip = slab // 2
    core = slab - 2 * chip
    other = (illum, slab + 1 - 2 * core)

    x, z = illum // 8, lax.rem(illum, 8)

    def illum_at(dx, dz):
        return lax.rem(x + dx, 4) * 8 + lax.rem(z + dz, 8)

    def slab_peer(k):
        return (illum, lax.rem(slab + k, NZ))

    def sent(src, dst, s_sem, r_sem, dev):
        return pltpu.make_async_remote_copy(
            src_ref=src, dst_ref=dst, send_sem=s_sem, recv_sem=r_sem, device_id=dev, device_id_type=MESH
        )

    def wait_bytes(ref, sem):
        pltpu.make_async_copy(ref, ref, sem).wait()

    barrier = pltpu.get_barrier_semaphore()

    def greet(peer):
        pl.semaphore_signal(barrier, inc=1, device_id=peer, device_id_type=MESH)

    for dz in DEPTH_STEPS:
        greet((illum_at(0, dz), slab))
    for dx in (2, 1, 3):
        for k in range(4):
            greet((illum_at(dx, 0), 4 * core + k))
    for k in range(1, NZ):
        greet(slab_peer(k))

    z_rows = pl.ds(pl.multiple_of(z * 8, 8), 8)
    loads = [
        pltpu.make_async_copy(src, dst, in_sem.at[i])
        for i, (src, dst) in enumerate((
            (block, zbuf.at[z_rows]), (angles_in, angles), (meas_in, meas), (dft_in, dft),
            (wg_in, wg), (source_table.at[slab], h7),
        ))
    ]
    for load in loads:
        load.start()
    for load in loads[:4]:
        load.wait()
    for q in (0, 1):
        for i, value in enumerate(split(dft[q])):
            right[q, i] = value
        for i, value in enumerate(split(dft[2 + q])):
            left[q, i] = value

    def store_mh(q, value):
        mh[q, 0] = value[:H]
        mh[q, 1] = value[H:]

    forward_plane(meas[0], meas[1], right, left, store_mh)
    pl.semaphore_wait(barrier, 7 + 12 + 7)

    for dz in DEPTH_STEPS:
        sent(zbuf.at[z_rows], zbuf.at[z_rows], ga_s, ga_r, (illum_at(0, dz), slab)).start()

    def angle_row(i):
        return jnp.sin(TILT * jnp.full((1, H), angles[0, i], jnp.int32).astype(jnp.float32))

    sine_x, sine_y = angle_row(0), angle_row(1)
    cos_z = jnp.sqrt(1.0 - sine_x * sine_x - sine_y * sine_y)
    x_at = lax.broadcasted_iota(jnp.int32, (N, H), 0).astype(jnp.float32)
    x_phase = WAVE * (sine_x * x_at)
    ex = jnp.cos(x_phase), jnp.sin(x_phase)
    y_at = lax.broadcasted_iota(jnp.int32, (1, H), 1).astype(jnp.float32)

    def incident(z):
        halves = []
        zf = jnp.full((1, H), z, jnp.int32).astype(jnp.float32)
        for q in (0, 1):
            phase = WAVE * (sine_y * (y_at + float(q * H)) + cos_z * zf)
            halves.append(cmul(ex, (jnp.cos(phase), jnp.sin(phase))))
        return tuple(jnp.concatenate([halves[0][i], halves[1][i]], axis=1) for i in (0, 1))

    def store_to(ref, p):
        def store(q, value):
            ref[p, q, 0] = value[:H]
            ref[p, q, 1] = value[H:]
        return store

    def load_from(ref, p):
        return lambda q: jnp.concatenate([ref[p, q, 0], ref[p, q, 1]], axis=0)

    def global_z(k):
        return k + core * (7 - 2 * k)

    def keep_incident(p):
        inc[p, 0], inc[p, 1] = incident(global_z(p))

    pl.loop(0, 4)(keep_incident)

    wait_bytes(zbuf.at[pl.ds(0, 56)], ga_r)

    high = slab // 4
    slot = slab + high * (7 - 2 * slab)
    x_rows = pl.ds(pl.multiple_of(x * 64, 64), 64)
    for dx, dy in CHIP_STEPS:
        dest = 2 * lax.rem(chip + dy, 4) + high
        sent(zbuf, c4.at[slot, x_rows], gb_s, gb_r.at[slot], (illum_at(dx, 0), dest)).start()

    def to_other():
        return sent(zbuf, c4.at[slot, x_rows], go_s, gb_r.at[slot], other)

    @pl.when(core != high)
    def _():
        to_other().start()

    @pl.when(core == high)
    def _():
        c4[slot, x_rows] = zbuf[...]

    def wait_plane(k):
        here = (core == high) & (slot == k)

        @pl.when(here)
        def _():
            wait_bytes(c4.at[k, pl.ds(0, 192)], gb_r.at[k])

        @pl.when(jnp.logical_not(here))
        def _():
            wait_bytes(c4.at[k], gb_r.at[k])

    everything = slice(None)

    def pair(ref, *at, rows=everything):
        return ref[(*at, 0, rows)], ref[(*at, 1, rows)]

    def put(ref, value, *at, rows=everything):
        ref[(*at, 0, rows)] = value[0]
        ref[(*at, 1, rows)] = value[1]

    def table(t, xp, sign, rows=everything):
        re, im = pair(wg, t, xp, rows=rows)
        return re, im if sign > 0 else -im

    def exchange(n, xp):
        return sent(f_buf.at[2, xp], ybuf.at[n, xp], x_s.at[n, xp], x_r.at[n, xp], other)

    def forward_chained(p, re, im, n, exact=True):
        def store(q, value):
            v = value[:H], value[H:]
            put(s_buf, v, p, q)
            if p:
                before = pair(s_buf, 0, q) if p == 1 else pair(f_buf, p - 2, q)
                put(f_buf, cadd(v, cmul(table(0, q, 1), before)), p - 1, q)
            if p == 3:
                exchange(n, q).start()

        forward_plane(re, im, right, left, store, exact)

    first = 2 * lax.rem(chip + core, 2)
    for i in range(4):
        p = lax.rem(first + i, 4)
        wait_plane(p)
        c = c4[p]
        forward_plane(c * inc[p, 0], c * inc[p, 1], right, left, store_to(s_buf, p))
    loads[4].wait()
    for xp in (0, 1):

        @pl.loop(0, H // 8)
        def _(i):
            rows = pl.ds(pl.multiple_of(i * 8, 8), 8)
            w = table(0, xp, 1, rows)
            f = pair(s_buf, 0, xp, rows=rows)
            for k in range(1, 4):
                f = cadd(pair(s_buf, k, xp, rows=rows), cmul(w, f))
                put(f_buf, f, k - 1, xp, rows=rows)

        exchange(0, xp).start()
    fields[0], fields[1] = incident(slab)

    def second_pass(src, n, sign, emit, acc):
        for xp in (0, 1):
            exchange(n, xp).wait()

            def step(i, acc):
                rows = pl.ds(pl.multiple_of(i * 8, 8), 8)
                w, g = table(0, xp, sign, rows), table(1, xp, sign, rows)
                t = pair(ybuf, n, xp, rows=rows)
                out = [None] * 4
                for k in (3, 2, 1, 0):
                    u = cmul(w, t)
                    v = pair(src, k, xp, rows=rows)
                    f = v if k == 0 else pair(f_buf, k - 1, xp, rows=rows)
                    out[k] = cmul(g, cadd(f, u))
                    if k:
                        t = cadd(v, u)
                return emit(out, xp, rows, acc)

            acc = lax.fori_loop(0, H // 8, step, acc)
            if emit.following is not None:
                exchange(emit.following, xp).start()
        return acc

    def inverse_back(src, n, keep):
        for xp in (0, 1):
            exchange(n, xp).wait()
        for p in (3, 2, 1, 0):

            def load(q):
                u = cmul(table(0, q, -1), pair(ybuf, n, q))
                v = pair(src, p, q)
                f = v if p == 0 else pair(f_buf, p - 1, q)
                if p:
                    put(ybuf, cadd(v, u), n, q)
                return jnp.concatenate(cmul(table(1, q, -1), cadd(f, u)), axis=0)

            keep(p, *inverse_plane(load, right, left))

    zero = jnp.zeros((8, N), jnp.float32)

    def norm(acc, value):
        return acc + (value[0] * value[0] + value[1] * value[1])

    def reduce_start(n, rows):
        for i, tile in enumerate(rows):
            red_out[n, i] = tile
        used = pl.ds(0, len(rows))
        copy = sent(red_out.at[n, used], red_in.at[n, used], rd_s.at[n], rd_r.at[n], other)
        copy.start()
        return copy

    def forward_chain(values, w, xp, rows):
        f = values[0]
        for k in range(1, 4):
            f = cadd(values[k], cmul(w, f))
            put(f_buf, f, k - 1, xp, rows=rows)

    def emit_first(out, xp, rows, acc):
        for k in range(4):
            put(w_buf, out[k], k, xp, rows=rows)
        forward_chain(out, table(0, xp, -1, rows), xp, rows)
        return acc

    emit_first.following = 1

    second_pass(s_buf, 0, 1, emit_first, 0)

    for p in range(4):
        re, im = inverse_plane(load_from(w_buf, p), right, left)
        r_buf[p, 0] = re
        r_buf[p, 1] = im

    square_sums = []

    def keep_gradient(p, re, im):
        c = c4[p]
        re = r_buf[p, 0] - c * re
        im = r_buf[p, 1] - c * im
        g0[p, 0] = re
        g0[p, 1] = im
        square_sums.append(tile_sum(re * re + im * im))

    inverse_back(w_buf, 1, keep_gradient)
    zz0 = sum(square_sums)
    for p in range(4):
        c = c4[p]
        forward_chained(p, c * g0[p, 0], c * g0[p, 1], 2)

    sender = chip // 2
    send_index = 2 * chip + 1 + sender * (6 - 4 * chip)
    own_index = jnp.where(core == sender, 2 * chip + sender * (6 - 4 * chip), 4)

    def plane_copy(n, ref):
        return sent(ref.at[send_index], ref.at[4], pg_s.at[n], pg_r.at[n], other)

    def hat_copy():
        return sent(gh0.at[0], gh0.at[4], ht_s.at[0], ht_r.at[0], other)

    def last_copy():
        return sent(g1.at[0], g1.at[5], ht_s.at[1], ht_r.at[1], other)

    @pl.when(core == sender)
    def _():
        plane_copy(0, g0).start()

    for p in range(4):
        forward_plane(g0[p, 0], g0[p, 1], right, left, store_to(gh0, p))

    @pl.when(core == 1)
    def _():
        hat_copy().start()

    def emit_image(out, xp, rows, acc):
        image = []
        for k in range(4):
            m = csub(pair(gh0, k, xp, rows=rows), out[k])
            acc = norm(acc, m)
            put(w_buf, m, k, xp, rows=rows)
            image.append(m)
        forward_chain(image, table(0, xp, -1, rows), xp, rows)
        return acc

    emit_image.following = 3
    mm0 = second_pass(s_buf, 2, 1, emit_image, zero)
    red0 = reduce_start(0, (zz0, tile_sum(mm0)))

    for p in range(4):
        re, im = inverse_plane(load_from(w_buf, p), right, left)
        r_buf[p, 0] = re
        r_buf[p, 1] = im

    red0.wait()
    zz_first = total_of(red_out[0, 0] + red_in[0, 0])
    mm_first = total_of(red_out[0, 1] + red_in[0, 1]) * (1.0 / (N * N))
    alpha0 = zz_first / mm_first

    square_sums = []

    def keep_next(p, re, im):
        c = c4[p]
        re = g0[p, 0] - alpha0 * (r_buf[p, 0] - c * re)
        im = g0[p, 1] - alpha0 * (r_buf[p, 1] - c * im)
        g1[p, 0] = re
        g1[p, 1] = im
        square_sums.append(tile_sum(re * re + im * im))

    inverse_back(w_buf, 3, keep_next)
    red1 = reduce_start(1, (sum(square_sums),))
    for p in range(4):
        c = c4[p]
        forward_chained(p, c * g1[p, 0], c * g1[p, 1], 4, exact=False)

    @pl.when(core == sender)
    def _():
        plane_copy(1, g1).start()

    for p in range(4):
        forward_plane(g1[p, 0], g1[p, 1], right, left, store_to(gh1, p), exact=False)

    @pl.when(core == 1)
    def _():
        last_copy().start()

    red1.wait()
    zz_second = total_of(red_out[1, 0] + red_in[1, 0])
    beta0 = zz_second / zz_first

    def emit_last(out, xp, rows, acc):
        for k in range(4):
            m = csub(pair(gh1, k, xp, rows=rows), out[k])
            old = pair(w_buf, k, xp, rows=rows)
            acc = norm(acc, (m[0] + beta0 * old[0], m[1] + beta0 * old[1]))
        return acc

    emit_last.following = None
    mm1 = second_pass(s_buf, 4, 1, emit_last, zero)
    red2 = reduce_start(2, (tile_sum(mm1),))

    @pl.when(core == sender)
    def _():
        plane_copy(0, g0).wait_send()
        plane_copy(1, g1).wait_send()

    @pl.when(core != sender)
    def _():
        plane_copy(0, g0).wait_recv()
        plane_copy(1, g1).wait_recv()

    @pl.when(core == 1)
    def _():
        hat_copy().wait_send()
        last_copy().wait_send()

    @pl.when(core == 0)
    def _():
        hat_copy().wait_recv()
        last_copy().wait_recv()

    loads[5].wait()
    last = 5 * (1 - core)
    forward_plane(g1[last, 0], g1[last, 1], right, left, store_to(gh1, 4))
    red2.wait()
    mm_second = total_of(red_out[2, 0] + red_in[2, 0]) * (1.0 / (N * N))
    alpha1 = zz_second / mm_second
    weight0 = alpha0 + alpha1 * beta0

    hat = 4 * (1 - core)
    for xp in (0, 1):
        s7 = tuple(weight0 * gh0[hat, xp, i] + alpha1 * gh1[4, xp, i] - mh[xp, i] for i in (0, 1))
        back = cmul((h7[xp, 0], h7[xp, 1]), s7)
        w_buf[0, xp, 0] = back[0]
        w_buf[0, xp, 1] = back[1]
    back_re, back_im = inverse_plane(load_from(w_buf, 0), right, left)
    more_re = weight0 * g0[own_index, 0] + alpha1 * g1[own_index, 0]
    more_im = weight0 * g0[own_index, 1] + alpha1 * g1[own_index, 1]
    sol_re = fields[0] + more_re
    sol_im = fields[1] + more_im
    fields[0] = sol_re
    fields[1] = sol_im
    part[...] = sol_re * back_re + sol_im * back_im

    for dx, dz in ILLUM_STEPS:
        peer = illum_at(dx, dz)
        rows = pl.ds(pl.multiple_of(peer * 8, 8), 8)
        sent(part.at[rows], rs_in.at[illum], rs_s, rs_r, (peer, slab)).start()
    rs_in[illum] = part[pl.ds(pl.multiple_of(illum * 8, 8), 8), :]
    miss_re = more_re - meas[0]
    miss_im = more_im - meas[1]
    misfit_tile = tile_sum(miss_re * miss_re + miss_im * miss_im)
    is_last = jnp.where(slab == NZ - 1, 0.5, 0.0)
    misfit_row = is_last * jnp.sum(misfit_tile, axis=0, keepdims=True)
    wait_bytes(rs_in.at[pl.ds(0, ILLUMS - 1)], rs_r)

    rows = jnp.sum(rs_in[...], axis=0)
    square_row = jnp.sum(tile_sum(rows * rows), axis=0, keepdims=True)
    lane = lax.broadcasted_iota(jnp.int32, (1, H), 1)
    both = jnp.where(
        lane < H // 2,
        square_row + pltpu.roll(square_row, H // 2, 1),
        misfit_row + pltpu.roll(misfit_row, H // 2, 1),
    )
    ar_out[0] = both
    pair_sum = sent(ar_out.at[0], ar_out.at[1], a1_s, a1_r, other)
    pair_sum.start()
    pair_sum.wait_recv()
    ar_out[2] = both + ar_out[1]
    me = illum * 4 + chip
    for dx, dz, dy in ALL_STEPS:
        peer = (illum_at(dx, dz), 2 * lax.rem(chip + dy, 4) + core)
        sent(ar_out.at[2], ar_in.at[me], a2_s, a2_r, peer).start()
    ar_in[me] = ar_out[2]
    wait_bytes(ar_in.at[pl.ds(0, CHIPS - 1)], a2_r)
    sums = jnp.sum(ar_in[...], axis=0)
    square = jnp.sum(jnp.where(lane < H // 2, sums, 0.0), axis=1, keepdims=True)
    descent[...] = rows / jnp.sqrt(square * (1.0 / (NZ * N * N)) + 1e-06)
    misfit[0, 0] = jnp.sum(jnp.where(lane < H // 2, 0.0, sums))

    wait_bytes(zbuf.at[pl.ds(0, 56)], ga_s)

    @pl.when(core != high)
    def _():
        to_other().wait_send()

    for _ in range(15):
        wait_bytes(zbuf, gb_s)
    wait_bytes(rs_in.at[pl.ds(0, ILLUMS - 1)], rs_s)
    pair_sum.wait_send()
    wait_bytes(ar_in.at[pl.ds(0, CHIPS - 1)], a2_s)


def body(angles, contrast, measured):
    dft = dft_tables()
    wg, source = depth_tables()
    vmem = pl.BlockSpec(memory_space=pltpu.VMEM)
    smem = pl.BlockSpec(memory_space=pltpu.SMEM)
    hbm = pl.BlockSpec(memory_space=pltpu.HBM)
    f32 = jnp.float32
    dma = pltpu.SemaphoreType.DMA
    spectral = (2, 2, H, N)
    fields, descent, misfit = pl.pallas_call(
        kernel,
        out_shape=(
            jax.ShapeDtypeStruct((2, N, N), f32),
            jax.ShapeDtypeStruct((8, N), f32),
            jax.ShapeDtypeStruct((1, 1), f32),
        ),
        in_specs=[hbm] * 6,
        out_specs=(vmem, vmem, smem),
        scratch_shapes=[
            pltpu.SMEM((1, 2), jnp.int32),
            pltpu.VMEM((2, N, N), f32),
            pltpu.VMEM((4, N, N), f32),
            pltpu.VMEM((2, 2, N, N), jnp.bfloat16),
            pltpu.VMEM((2, 2, N, N), jnp.bfloat16),
            pltpu.VMEM((2, *spectral), f32),
            pltpu.VMEM((4, 2, N, N), f32),
            pltpu.VMEM((64, N), f32),
            pltpu.VMEM((4, N, N), f32),
            pltpu.VMEM((4, *spectral), f32),
            pltpu.VMEM((3, *spectral), f32),
            pltpu.VMEM((4, *spectral), f32),
            pltpu.VMEM((5, *spectral), f32),
            pltpu.VMEM((5, *spectral), f32),
            pltpu.VMEM((5, 2, N, N), f32),
            pltpu.VMEM((6, 2, N, N), f32),
            pltpu.VMEM((4, 2, N, N), f32),
            pltpu.VMEM((5, *spectral), f32),
            pltpu.VMEM((3, 2, 8, H), f32),
            pltpu.VMEM((3, 2, 8, H), f32),
            pltpu.VMEM(spectral, f32),
            pltpu.VMEM(spectral, f32),
            pltpu.VMEM((N, N), f32),
            pltpu.VMEM((ILLUMS, 8, N), f32),
            pltpu.VMEM((3, 1, H), f32),
            pltpu.VMEM((CHIPS, 1, H), f32),
            dma((6,)), dma, dma, dma, dma, dma((4,)),
            dma((5, 2)), dma((5, 2)),
            dma((3,)), dma((3,)), dma((2,)), dma((2,)), dma((2,)), dma((2,)),
            dma, dma, dma, dma, dma, dma,
        ],
        compiler_params=pltpu.CompilerParams(
            collective_id=0, has_side_effects=True, vmem_limit_bytes=53 * 1024 * 1024,
        ),
    )(
        angles, contrast.reshape(8, N), measured.reshape(2, N, N),
        jnp.asarray(dft), jnp.asarray(wg), jnp.asarray(source),
    )
    return fields.reshape(1, 2, 1, N, N), descent.reshape(1, 8, N), misfit.reshape(())


def solution(mesh):
    return jax.shard_map(
        body,
        mesh=mesh,
        in_specs=(P("illum", None), P("slab", "illum", None), P("illum", None, None, None)),
        out_specs=(P("illum", None, "slab", None, None), P("slab", "illum", None), P()),
        check_vma=False,
    )
```

```python
import itertools
import math

import jax
import jax.numpy as jnp
import ml_dtypes
import numpy as np
from jax import lax
from jax.experimental import pallas as pl
from jax.experimental.pallas import tpu as pltpu
from jax.sharding import PartitionSpec as P

MESH = pl.DeviceIdType.MESH
N = 256
H = 128
NZ = 8
ILLUMS = 32
WAVE = 2.0 * math.pi / 8.0
DAMPING = 0.2
TILT = 0.04


def far_first(*sizes):
    def length(step):
        return sum(min(k, n - k) for k, n in zip(step, sizes))

    steps = [step for step in itertools.product(*map(range, sizes)) if any(step)]
    return sorted(steps, key=length, reverse=True)


ILLUM_STEPS = far_first(4, 8)
EARLY_STEPS = [(dx, dy) for dy in (2, 0) for dx in (2, 1, 3, 0) if dx or dy]
LATE_STEPS = [(dx, dy) for dy in (1, 3) for dx in (2, 1, 3, 0)]
ALL_STEPS = far_first(4, 8, 4)
CHIPS = 128
DEPTH_STEPS = sorted(range(1, 8), key=lambda k: -min(k, 8 - k))


def balanced(c, s):
    exact = c + 1j * s
    near = [v.astype(ml_dtypes.bfloat16).astype(np.float64) for v in (c, s)]
    step = [2.0 ** (np.floor(np.log2(np.maximum(np.abs(v), 1e-30))) - 7) for v in (c, s)]
    away = [n + np.sign(v - n) * d for v, n, d in zip((c, s), near, step)]
    away = [a.astype(ml_dtypes.bfloat16).astype(np.float64) for a in away]
    out = near[0] + 1j * near[1]
    change = np.concatenate([away[0] - near[0], 1j * (away[1] - near[1])]) * np.conj(np.concatenate([exact, exact]))
    flipped = np.zeros(change.shape, bool)
    for m in range(c.shape[1]):
        bias = np.sum((out[:, m] - exact[:, m]) * np.conj(exact[:, m]))
        for _ in range(24):
            trial = np.abs(bias + np.where(flipped[:, m], np.inf, change[:, m].real) + 1j * change[:, m].imag)
            best = np.argmin(trial)
            if not trial[best] < np.abs(bias):
                break
            flipped[best, m] = True
            bias = bias + change[best, m]
    real, imag = flipped[: c.shape[0]], flipped[c.shape[0] :]
    return np.where(real, away[0], near[0]), np.where(imag, away[1], near[1])


def dft_tables():
    n = np.arange(H)[:, None]
    m = np.arange(H)[None, :]
    out, light = [], []
    for q in (0, 1):
        theta = -2.0 * np.pi / N * ((n * (2 * m + q)) % N)
        c, s = np.cos(theta), np.sin(theta)
        out.append(np.block([[c, s], [-s, c]]))
        c, s = balanced(c, s)
        light.append(np.block([[c, s], [-s, c]]))
    return np.stack(out + [r.T for r in out] + light + [r.T for r in light]).astype(np.float32)


def depth_tables():
    order = np.concatenate([np.arange(0, N, 2), np.arange(1, N, 2)])
    sym = 2.0 - 2.0 * np.cos(2.0 * np.pi / N * order)
    b = WAVE * WAVE
    p = sym[:, None] + sym[None, :] - b
    l = b * DAMPING
    r = np.sqrt(p * p + l * l)
    qr = np.sqrt((r + p) / 2.0)
    qi = l / (2.0 * qr)
    w = np.exp(-(qr + 1j * qi))
    g = b / (2.0 * r) * (qr - 1j * qi)

    def pack(t):
        t = t.reshape(2, H, N)
        return np.stack([t.real, t.imag], axis=1).astype(np.float32)

    source = np.stack([pack(np.conj(g * w ** (NZ - 1 - s))) for s in range(NZ)])
    return np.stack([pack(w), pack(g)]), source


def split(a):
    hi = a.astype(jnp.bfloat16)
    lo = (a - hi.astype(jnp.float32)).astype(jnp.bfloat16)
    return hi, lo


def dot_right(a, m_ref, q, exact=True):
    if not exact:
        return jnp.dot(a.astype(jnp.bfloat16), m_ref[q, 2], preferred_element_type=jnp.float32)
    hi, lo = split(a)
    mh, ml = m_ref[q, 0], m_ref[q, 1]
    return jnp.dot(
        jnp.concatenate([hi, lo, hi], axis=1),
        jnp.concatenate([mh, mh, ml], axis=0),
        preferred_element_type=jnp.float32,
    )


def dot_left(m_ref, q, a, exact=True):
    if not exact:
        return jnp.dot(m_ref[q, 2], a.astype(jnp.bfloat16), preferred_element_type=jnp.float32)
    hi, lo = split(a)
    mh, ml = m_ref[q, 0], m_ref[q, 1]
    return jnp.dot(
        jnp.concatenate([mh, mh, ml], axis=1),
        jnp.concatenate([hi, lo, hi], axis=0),
        preferred_element_type=jnp.float32,
    )


def forward_plane(re, im, right, left, store, exact=True):
    halves = []
    for q in (0, 1):
        if q == 0:
            a = jnp.concatenate([re[:, :H] + re[:, H:], im[:, :H] + im[:, H:]], axis=1)
        else:
            a = jnp.concatenate([re[:, :H] - re[:, H:], im[:, :H] - im[:, H:]], axis=1)
        halves.append(dot_right(a, right, q, exact))
    for q in (0, 1):
        parts = []
        for t in halves:
            u = t[:H] + t[H:] if q == 0 else t[:H] - t[H:]
            parts.append(jnp.concatenate([u[:, :H], u[:, H:]], axis=0))
        store(q, dot_left(left, q, jnp.concatenate(parts, axis=1), exact))


def inverse_plane(load, right, left):
    e = [dot_left(right, q, load(q)) for q in (0, 1)]
    e = [part * (1.0 / (N * N)) for part in e]
    top, bottom = e[0] + e[1], e[0] - e[1]
    re = jnp.concatenate([top[:H], bottom[:H]], axis=0)
    im = jnp.concatenate([top[H:], bottom[H:]], axis=0)
    e = []
    for q in (0, 1):
        z = jnp.concatenate([re[:, q * H : (q + 1) * H], im[:, q * H : (q + 1) * H]], axis=1)
        e.append(dot_right(z, left, q))
    low, high = e[0] + e[1], e[0] - e[1]
    re = jnp.concatenate([low[:, :H], high[:, :H]], axis=1)
    im = jnp.concatenate([low[:, H:], high[:, H:]], axis=1)
    return re, im


def cmul(a, b):
    return a[0] * b[0] - a[1] * b[1], a[0] * b[1] + a[1] * b[0]


def cadd(a, b):
    return a[0] + b[0], a[1] + b[1]


def csub(a, b):
    return a[0] - b[0], a[1] - b[1]


def tile_sum(a):
    a = a[:, :H] + a[:, H:]
    if a.shape[0] > 8:
        a = jnp.sum(a.reshape(a.shape[0] // 8, 8, H), axis=0)
    return a


def total_of(tile):
    return jnp.sum(jnp.sum(tile, axis=0, keepdims=True), axis=1, keepdims=True)


def kernel(
    angles_in, block, meas_in, dft_in, wg_in, source_table,
    fields, descent, misfit,
    angles, meas, dft, right, left, wg, inc, zbuf, c4, s_buf, f_buf, w_buf, gh0, gh1, g0, g1, r_buf, ybuf, red_out, red_in,
    mh, h7, part, rs_in, ar_out, ar_in,
    in_sem, ga_s, ga_r, gb_s, go_s, gb_r, x_s, x_r, rd_s, rd_r, pg_s, pg_r, ht_s, ht_r,
    rs_s, rs_r, a1_s, a1_r, a2_s, a2_r,
):
    illum = lax.axis_index("illum")
    slab = lax.axis_index("slab")
    chip = slab // 2
    core = slab - 2 * chip
    other = (illum, slab + 1 - 2 * core)

    x, z = illum // 8, lax.rem(illum, 8)

    def illum_at(dx, dz):
        return lax.rem(x + dx, 4) * 8 + lax.rem(z + dz, 8)

    def slab_peer(k):
        return (illum, lax.rem(slab + k, NZ))

    def sent(src, dst, s_sem, r_sem, dev):
        return pltpu.make_async_remote_copy(
            src_ref=src, dst_ref=dst, send_sem=s_sem, recv_sem=r_sem, device_id=dev, device_id_type=MESH
        )

    def wait_bytes(ref, sem):
        pltpu.make_async_copy(ref, ref, sem).wait()

    barrier = pltpu.get_barrier_semaphore()

    def greet(peer):
        pl.semaphore_signal(barrier, inc=1, device_id=peer, device_id_type=MESH)

    for dz in DEPTH_STEPS:
        greet((illum_at(0, dz), slab))
    for dx in (2, 1, 3):
        for k in range(4):
            greet((illum_at(dx, 0), 4 * core + k))
    for k in range(1, NZ):
        greet(slab_peer(k))

    loads = [
        pltpu.make_async_copy(src, dst, in_sem.at[i])
        for i, (src, dst) in enumerate((
            (angles_in, angles), (dft_in, dft), (meas_in, meas),
            (wg_in, wg), (source_table.at[slab], h7),
        ))
    ]
    for load in loads:
        load.start()
    pl.semaphore_wait(barrier, 7 + 12 + 7)

    high = slab // 4
    slot = slab + high * (7 - 2 * slab)

    def z_rows(k, n):
        return pl.ds(pl.multiple_of(k * n, n), n)

    def chip_peer(dx, dy):
        return (illum_at(dx, 0), 2 * lax.rem(chip + dy, 4) + high)

    for dz in DEPTH_STEPS:
        sent(block, zbuf.at[z_rows(z, 8)], ga_s, ga_r.at[z], (illum_at(0, dz), slab)).start()
    own_rows = pltpu.make_async_copy(block, zbuf.at[z_rows(z, 8)], ga_r.at[z])
    own_rows.start()

    def pass_on(step):
        k = lax.rem(z // 2 + 4 + step, 4)
        for i in (0, 1):
            pltpu.make_async_copy(block, zbuf.at[z_rows(2 * k + i, 8)], ga_r.at[2 * k + i]).wait()
        for dx, dy in EARLY_STEPS:
            rows = pl.ds(pl.multiple_of(x * 64 + k * 16, 16), 16)
            sent(zbuf.at[z_rows(k, 16)], c4.at[slot, rows], gb_s, gb_r.at[slot], chip_peer(dx, dy)).start()

    near = 2 * lax.rem(z, 2) - 1
    loads[0].wait()

    def angle_row(i):
        return jnp.sin(TILT * jnp.full((1, H), angles[0, i], jnp.int32).astype(jnp.float32))

    sine_x, sine_y = angle_row(0), angle_row(1)
    cos_z = jnp.sqrt(1.0 - sine_x * sine_x - sine_y * sine_y)
    x_at = lax.broadcasted_iota(jnp.int32, (N, H), 0).astype(jnp.float32)
    x_phase = WAVE * (sine_x * x_at)
    ex = jnp.cos(x_phase), jnp.sin(x_phase)
    y_at = lax.broadcasted_iota(jnp.int32, (1, H), 1).astype(jnp.float32)

    def incident(z):
        halves = []
        zf = jnp.full((1, H), z, jnp.int32).astype(jnp.float32)
        for q in (0, 1):
            phase = WAVE * (sine_y * (y_at + float(q * H)) + cos_z * zf)
            halves.append(cmul(ex, (jnp.cos(phase), jnp.sin(phase))))
        return tuple(jnp.concatenate([halves[0][i], halves[1][i]], axis=1) for i in (0, 1))

    def store_to(ref, p):
        def store(q, value):
            ref[p, q, 0] = value[:H]
            ref[p, q, 1] = value[H:]
        return store

    def load_from(ref, p):
        return lambda q: jnp.concatenate([ref[p, q, 0], ref[p, q, 1]], axis=0)

    def global_z(k):
        return k + core * (7 - 2 * k)

    def keep_incident(p):
        inc[p, 0], inc[p, 1] = incident(global_z(p))

    pl.loop(0, 4)(keep_incident)

    pass_on(0)
    pass_on(near)

    def store_mh(q, value):
        mh[q, 0] = value[:H]
        mh[q, 1] = value[H:]

    for load in loads[1:3]:
        load.wait()
    for q in (0, 1):
        for i, value in enumerate(split(dft[q])):
            right[q, i] = value
        for i, value in enumerate(split(dft[2 + q])):
            left[q, i] = value
        right[q, 2] = dft[4 + q].astype(jnp.bfloat16)
        left[q, 2] = dft[6 + q].astype(jnp.bfloat16)
    pass_on(-near)
    forward_plane(meas[0], meas[1], right, left, store_mh)
    pass_on(2)

    all_rows = pl.ds(pl.multiple_of(x * 64, 64), 64)
    for dx, dy in LATE_STEPS:
        sent(zbuf, c4.at[slot, all_rows], gb_s, gb_r.at[slot], chip_peer(dx, dy)).start()

    def to_other():
        return sent(zbuf, c4.at[slot, all_rows], go_s, gb_r.at[slot], other)

    @pl.when(core != high)
    def _():
        to_other().start()

    @pl.when(core == high)
    def _():
        c4[slot, all_rows] = zbuf[...]

    def wait_plane(k):
        here = (core == high) & (slot == k)

        @pl.when(here)
        def _():
            wait_bytes(c4.at[k, pl.ds(0, 192)], gb_r.at[k])

        @pl.when(jnp.logical_not(here))
        def _():
            wait_bytes(c4.at[k], gb_r.at[k])

    everything = slice(None)

    def pair(ref, *at, rows=everything):
        return ref[(*at, 0, rows)], ref[(*at, 1, rows)]

    def put(ref, value, *at, rows=everything):
        ref[(*at, 0, rows)] = value[0]
        ref[(*at, 1, rows)] = value[1]

    def table(t, xp, sign, rows=everything):
        re, im = pair(wg, t, xp, rows=rows)
        return re, im if sign > 0 else -im

    def chunks(n):
        size = H // 2 if n == 0 else H
        return [(xp, base, size) for xp in (0, 1) for base in range(0, H, size)]

    def exchange(n, q):
        xp, base, size = chunks(n)[q]
        rows = pl.ds(base, size)
        return sent(f_buf.at[2, xp, :, rows], ybuf.at[n, xp, :, rows], x_s.at[n, q], x_r.at[n, q], other)

    def forward_chained(p, re, im, n, exact=True):
        def store(q, value):
            v = value[:H], value[H:]
            put(s_buf, v, p, q)
            if p:
                before = pair(s_buf, 0, q) if p == 1 else pair(f_buf, p - 2, q)
                put(f_buf, cadd(v, cmul(table(0, q, 1), before)), p - 1, q)
            if p == 3:
                exchange(n, q).start()

        forward_plane(re, im, right, left, store, exact)

    first = 2 * lax.rem(chip + core, 2)
    for i in range(4):
        p = lax.rem(first + i, 4)
        wait_plane(p)
        c = c4[p]
        forward_plane(c * inc[p, 0], c * inc[p, 1], right, left, store_to(s_buf, p))
    loads[3].wait()
    for q, (xp, base, size) in enumerate(chunks(0)):

        @pl.loop(0, size // 16)
        def _(i):
            rows = pl.ds(pl.multiple_of(base + i * 16, 16), 16)
            w = table(0, xp, 1, rows)
            f = pair(s_buf, 0, xp, rows=rows)
            for k in range(1, 4):
                f = cadd(pair(s_buf, k, xp, rows=rows), cmul(w, f))
                put(f_buf, f, k - 1, xp, rows=rows)

        exchange(0, q).start()
    fields[0], fields[1] = incident(slab)

    def second_pass(src, n, sign, emit, acc):
        for q, (xp, base, size) in enumerate(chunks(n)):
            exchange(n, q).wait()

            def step(i, acc):
                rows = pl.ds(pl.multiple_of(base + i * 16, 16), 16)
                w, g = table(0, xp, sign, rows), table(1, xp, sign, rows)
                t = pair(ybuf, n, xp, rows=rows)
                out = [None] * 4
                for k in (3, 2, 1, 0):
                    u = cmul(w, t)
                    v = pair(src, k, xp, rows=rows)
                    f = v if k == 0 else pair(f_buf, k - 1, xp, rows=rows)
                    out[k] = cmul(g, cadd(f, u))
                    if k:
                        t = cadd(v, u)
                return emit(out, xp, rows, acc)

            acc = lax.fori_loop(0, size // 16, step, acc)
            if emit.following is not None and base + size == H:
                exchange(emit.following, xp).start()
        return acc

    def inverse_back(src, n, keep):
        for xp in (0, 1):
            exchange(n, xp).wait()
        for p in (3, 2, 1, 0):

            def load(q):
                u = cmul(table(0, q, -1), pair(ybuf, n, q))
                v = pair(src, p, q)
                f = v if p == 0 else pair(f_buf, p - 1, q)
                if p:
                    put(ybuf, cadd(v, u), n, q)
                return jnp.concatenate(cmul(table(1, q, -1), cadd(f, u)), axis=0)

            keep(p, *inverse_plane(load, right, left))

    zero = jnp.zeros((16, N), jnp.float32)

    def norm(acc, value):
        return acc + (value[0] * value[0] + value[1] * value[1])

    def reduce_start(n, rows):
        for i, tile in enumerate(rows):
            red_out[n, i] = tile
        used = pl.ds(0, len(rows))
        copy = sent(red_out.at[n, used], red_in.at[n, used], rd_s.at[n], rd_r.at[n], other)
        copy.start()
        return copy

    def forward_chain(values, w, xp, rows):
        f = values[0]
        for k in range(1, 4):
            f = cadd(values[k], cmul(w, f))
            put(f_buf, f, k - 1, xp, rows=rows)

    def emit_first(out, xp, rows, acc):
        for k in range(4):
            put(w_buf, out[k], k, xp, rows=rows)
        forward_chain(out, table(0, xp, -1, rows), xp, rows)
        return acc

    emit_first.following = 1

    second_pass(s_buf, 0, 1, emit_first, 0)

    for p in range(4):
        re, im = inverse_plane(load_from(w_buf, p), right, left)
        r_buf[p, 0] = re
        r_buf[p, 1] = im

    square_sums = []

    def keep_gradient(p, re, im):
        c = c4[p]
        re = r_buf[p, 0] - c * re
        im = r_buf[p, 1] - c * im
        g0[p, 0] = re
        g0[p, 1] = im
        square_sums.append(tile_sum(re * re + im * im))

    inverse_back(w_buf, 1, keep_gradient)
    zz0 = sum(square_sums)
    for p in range(4):
        c = c4[p]
        forward_chained(p, c * g0[p, 0], c * g0[p, 1], 2)

    sender = chip // 2
    send_index = 2 * chip + 1 + sender * (6 - 4 * chip)
    own_index = jnp.where(core == sender, 2 * chip + sender * (6 - 4 * chip), 4)

    def plane_copy(n, ref):
        return sent(ref.at[send_index], ref.at[4], pg_s.at[n], pg_r.at[n], other)

    def hat_copy():
        return sent(gh0.at[0], gh0.at[4], ht_s.at[0], ht_r.at[0], other)

    def last_copy():
        return sent(g1.at[0], g1.at[5], ht_s.at[1], ht_r.at[1], other)

    @pl.when(core == sender)
    def _():
        plane_copy(0, g0).start()

    for p in range(4):
        forward_plane(g0[p, 0], g0[p, 1], right, left, store_to(gh0, p))

    @pl.when(core == 1)
    def _():
        hat_copy().start()

    def emit_image(out, xp, rows, acc):
        image = []
        for k in range(4):
            m = csub(pair(gh0, k, xp, rows=rows), out[k])
            acc = norm(acc, m)
            put(w_buf, m, k, xp, rows=rows)
            image.append(m)
        forward_chain(image, table(0, xp, -1, rows), xp, rows)
        return acc

    emit_image.following = 3
    mm0 = second_pass(s_buf, 2, 1, emit_image, zero)
    red0 = reduce_start(0, (zz0, tile_sum(mm0)))

    for p in range(4):
        re, im = inverse_plane(load_from(w_buf, p), right, left)
        r_buf[p, 0] = re
        r_buf[p, 1] = im

    red0.wait()
    zz_first = total_of(red_out[0, 0] + red_in[0, 0])
    mm_first = total_of(red_out[0, 1] + red_in[0, 1]) * (1.0 / (N * N))
    alpha0 = zz_first / mm_first

    square_sums = []

    def keep_next(p, re, im):
        c = c4[p]
        re = g0[p, 0] - alpha0 * (r_buf[p, 0] - c * re)
        im = g0[p, 1] - alpha0 * (r_buf[p, 1] - c * im)
        g1[p, 0] = re
        g1[p, 1] = im
        square_sums.append(tile_sum(re * re + im * im))

    inverse_back(w_buf, 3, keep_next)
    red1 = reduce_start(1, (sum(square_sums),))
    for p in range(4):
        c = c4[p]
        forward_chained(p, c * g1[p, 0], c * g1[p, 1], 4, exact=False)

    @pl.when(core == sender)
    def _():
        plane_copy(1, g1).start()

    for p in range(4):
        forward_plane(g1[p, 0], g1[p, 1], right, left, store_to(gh1, p), exact=False)

    @pl.when(core == 1)
    def _():
        last_copy().start()

    red1.wait()
    zz_second = total_of(red_out[1, 0] + red_in[1, 0])
    beta0 = zz_second / zz_first

    def emit_last(out, xp, rows, acc):
        for k in range(4):
            m = csub(pair(gh1, k, xp, rows=rows), out[k])
            old = pair(w_buf, k, xp, rows=rows)
            acc = norm(acc, (m[0] + beta0 * old[0], m[1] + beta0 * old[1]))
        return acc

    emit_last.following = None
    mm1 = second_pass(s_buf, 4, 1, emit_last, zero)
    red2 = reduce_start(2, (tile_sum(mm1),))

    @pl.when(core == sender)
    def _():
        plane_copy(0, g0).wait_send()
        plane_copy(1, g1).wait_send()

    @pl.when(core != sender)
    def _():
        plane_copy(0, g0).wait_recv()
        plane_copy(1, g1).wait_recv()

    @pl.when(core == 1)
    def _():
        hat_copy().wait_send()
        last_copy().wait_send()

    @pl.when(core == 0)
    def _():
        hat_copy().wait_recv()
        last_copy().wait_recv()

    loads[4].wait()
    last = 5 * (1 - core)
    forward_plane(g1[last, 0], g1[last, 1], right, left, store_to(gh1, 4))
    red2.wait()
    mm_second = total_of(red_out[2, 0] + red_in[2, 0]) * (1.0 / (N * N))
    alpha1 = zz_second / mm_second
    weight0 = alpha0 + alpha1 * beta0

    hat = 4 * (1 - core)
    for xp in (0, 1):
        s7 = tuple(weight0 * gh0[hat, xp, i] + alpha1 * gh1[4, xp, i] - mh[xp, i] for i in (0, 1))
        back = cmul((h7[xp, 0], h7[xp, 1]), s7)
        w_buf[0, xp, 0] = back[0]
        w_buf[0, xp, 1] = back[1]
    back_re, back_im = inverse_plane(load_from(w_buf, 0), right, left)
    more_re = weight0 * g0[own_index, 0] + alpha1 * g1[own_index, 0]
    more_im = weight0 * g0[own_index, 1] + alpha1 * g1[own_index, 1]
    sol_re = fields[0] + more_re
    sol_im = fields[1] + more_im
    fields[0] = sol_re
    fields[1] = sol_im
    part[...] = sol_re * back_re + sol_im * back_im

    for dx, dz in ILLUM_STEPS:
        peer = illum_at(dx, dz)
        rows = pl.ds(pl.multiple_of(peer * 8, 8), 8)
        sent(part.at[rows], rs_in.at[illum], rs_s, rs_r, (peer, slab)).start()
    rs_in[illum] = part[pl.ds(pl.multiple_of(illum * 8, 8), 8), :]
    miss_re = more_re - meas[0]
    miss_im = more_im - meas[1]
    misfit_tile = tile_sum(miss_re * miss_re + miss_im * miss_im)
    is_last = jnp.where(slab == NZ - 1, 0.5, 0.0)
    misfit_row = is_last * jnp.sum(misfit_tile, axis=0, keepdims=True)
    wait_bytes(rs_in.at[pl.ds(0, ILLUMS - 1)], rs_r)

    rows = jnp.sum(rs_in[...], axis=0)
    square_row = jnp.sum(tile_sum(rows * rows), axis=0, keepdims=True)
    lane = lax.broadcasted_iota(jnp.int32, (1, H), 1)
    both = jnp.where(
        lane < H // 2,
        square_row + pltpu.roll(square_row, H // 2, 1),
        misfit_row + pltpu.roll(misfit_row, H // 2, 1),
    )
    ar_out[0] = both
    pair_sum = sent(ar_out.at[0], ar_out.at[1], a1_s, a1_r, other)
    pair_sum.start()
    pair_sum.wait_recv()
    ar_out[2] = both + ar_out[1]
    me = illum * 4 + chip
    for dx, dz, dy in ALL_STEPS:
        peer = (illum_at(dx, dz), 2 * lax.rem(chip + dy, 4) + core)
        sent(ar_out.at[2], ar_in.at[me], a2_s, a2_r, peer).start()
    ar_in[me] = ar_out[2]
    wait_bytes(ar_in.at[pl.ds(0, CHIPS - 1)], a2_r)
    sums = jnp.sum(ar_in[...], axis=0)
    square = jnp.sum(jnp.where(lane < H // 2, sums, 0.0), axis=1, keepdims=True)
    descent[...] = rows / jnp.sqrt(square * (1.0 / (NZ * N * N)) + 1e-06)
    misfit[0, 0] = jnp.sum(jnp.where(lane < H // 2, 0.0, sums))

    wait_bytes(zbuf.at[pl.ds(0, 56)], ga_s)

    @pl.when(core != high)
    def _():
        to_other().wait_send()

    for _ in range(15):
        wait_bytes(zbuf, gb_s)
    wait_bytes(rs_in.at[pl.ds(0, ILLUMS - 1)], rs_s)
    pair_sum.wait_send()
    wait_bytes(ar_in.at[pl.ds(0, CHIPS - 1)], a2_s)


def body(angles, contrast, measured):
    dft = dft_tables()
    wg, source = depth_tables()
    vmem = pl.BlockSpec(memory_space=pltpu.VMEM)
    smem = pl.BlockSpec(memory_space=pltpu.SMEM)
    hbm = pl.BlockSpec(memory_space=pltpu.HBM)
    f32 = jnp.float32
    dma = pltpu.SemaphoreType.DMA
    spectral = (2, 2, H, N)
    fields, descent, misfit = pl.pallas_call(
        kernel,
        out_shape=(
            jax.ShapeDtypeStruct((2, N, N), f32),
            jax.ShapeDtypeStruct((8, N), f32),
            jax.ShapeDtypeStruct((1, 1), f32),
        ),
        in_specs=[hbm] * 6,
        out_specs=(vmem, vmem, smem),
        scratch_shapes=[
            pltpu.SMEM((1, 2), jnp.int32),
            pltpu.VMEM((2, N, N), f32),
            pltpu.VMEM((8, N, N), f32),
            pltpu.VMEM((2, 3, N, N), jnp.bfloat16),
            pltpu.VMEM((2, 3, N, N), jnp.bfloat16),
            pltpu.VMEM((2, *spectral), f32),
            pltpu.VMEM((4, 2, N, N), f32),
            pltpu.VMEM((64, N), f32),
            pltpu.VMEM((4, N, N), f32),
            pltpu.VMEM((4, *spectral), f32),
            pltpu.VMEM((3, *spectral), f32),
            pltpu.VMEM((4, *spectral), f32),
            pltpu.VMEM((5, *spectral), f32),
            pltpu.VMEM((5, *spectral), f32),
            pltpu.VMEM((5, 2, N, N), f32),
            pltpu.VMEM((6, 2, N, N), f32),
            pltpu.VMEM((4, 2, N, N), f32),
            pltpu.VMEM((5, *spectral), f32),
            pltpu.VMEM((3, 2, 8, H), f32),
            pltpu.VMEM((3, 2, 8, H), f32),
            pltpu.VMEM(spectral, f32),
            pltpu.VMEM(spectral, f32),
            pltpu.VMEM((N, N), f32),
            pltpu.VMEM((ILLUMS, 8, N), f32),
            pltpu.VMEM((3, 1, H), f32),
            pltpu.VMEM((CHIPS, 1, H), f32),
            dma((5,)), dma, dma((8,)), dma, dma, dma((4,)),
            dma((5, 4)), dma((5, 4)),
            dma((3,)), dma((3,)), dma((2,)), dma((2,)), dma((2,)), dma((2,)),
            dma, dma, dma, dma, dma, dma,
        ],
        compiler_params=pltpu.CompilerParams(
            collective_id=0, has_side_effects=True, vmem_limit_bytes=53 * 1024 * 1024,
        ),
    )(
        angles, contrast.reshape(8, N), measured.reshape(2, N, N),
        jnp.asarray(dft), jnp.asarray(wg), jnp.asarray(source),
    )
    return fields.reshape(1, 2, 1, N, N), descent.reshape(1, 8, N), misfit.reshape(())


def solution(mesh):
    return jax.shard_map(
        body,
        mesh=mesh,
        in_specs=(P("illum", None), P("slab", "illum", None), P("illum", None, None, None)),
        out_specs=(P("illum", None, "slab", None, None), P("slab", "illum", None), P()),
        check_vma=False,
    )
```

```python
import itertools
import math

import jax
import jax.numpy as jnp
import ml_dtypes
import numpy as np
from jax import lax
from jax.experimental import pallas as pl
from jax.experimental.pallas import tpu as pltpu
from jax.sharding import PartitionSpec as P

MESH = pl.DeviceIdType.MESH
N = 256
H = 128
NZ = 8
ILLUMS = 32
WAVE = 2.0 * math.pi / 8.0
DAMPING = 0.2
TILT = 0.04


def far_first(*sizes):
    def length(step):
        return sum(min(k, n - k) for k, n in zip(step, sizes))

    steps = [step for step in itertools.product(*map(range, sizes)) if any(step)]
    return sorted(steps, key=length, reverse=True)


ILLUM_STEPS = far_first(4, 8)
EARLY_STEPS = [(dx, dy) for dy in (2, 0) for dx in (2, 1, 3, 0) if dx or dy]
LATE_STEPS = [(dx, dy) for dy in (1, 3) for dx in (2, 1, 3, 0)]
ALL_STEPS = far_first(4, 8, 4, 2)
DEVICES = 256
DEPTH_STEPS = sorted(range(1, 8), key=lambda k: -min(k, 8 - k))


def balanced(c, s):
    exact = c + 1j * s
    near = [v.astype(ml_dtypes.bfloat16).astype(np.float64) for v in (c, s)]
    step = [2.0 ** (np.floor(np.log2(np.maximum(np.abs(v), 1e-30))) - 7) for v in (c, s)]
    away = [n + np.sign(v - n) * d for v, n, d in zip((c, s), near, step)]
    away = [a.astype(ml_dtypes.bfloat16).astype(np.float64) for a in away]
    out = near[0] + 1j * near[1]
    change = np.concatenate([away[0] - near[0], 1j * (away[1] - near[1])]) * np.conj(np.concatenate([exact, exact]))
    flipped = np.zeros(change.shape, bool)
    for m in range(c.shape[1]):
        bias = np.sum((out[:, m] - exact[:, m]) * np.conj(exact[:, m]))
        for _ in range(24):
            trial = np.abs(bias + np.where(flipped[:, m], np.inf, change[:, m].real) + 1j * change[:, m].imag)
            best = np.argmin(trial)
            if not trial[best] < np.abs(bias):
                break
            flipped[best, m] = True
            bias = bias + change[best, m]
    real, imag = flipped[: c.shape[0]], flipped[c.shape[0] :]
    return np.where(real, away[0], near[0]), np.where(imag, away[1], near[1])


def dft_tables():
    n = np.arange(H)[:, None]
    m = np.arange(H)[None, :]
    out, light = [], []
    for q in (0, 1):
        theta = -2.0 * np.pi / N * ((n * (2 * m + q)) % N)
        c, s = np.cos(theta), np.sin(theta)
        out.append(np.block([[c, s], [-s, c]]))
        c, s = balanced(c, s)
        light.append(np.block([[c, s], [-s, c]]))
    return np.stack(out + [r.T for r in out] + light + [r.T for r in light]).astype(np.float32)


def depth_tables():
    order = np.concatenate([np.arange(0, N, 2), np.arange(1, N, 2)])
    sym = 2.0 - 2.0 * np.cos(2.0 * np.pi / N * order)
    b = WAVE * WAVE
    p = sym[:, None] + sym[None, :] - b
    l = b * DAMPING
    r = np.sqrt(p * p + l * l)
    qr = np.sqrt((r + p) / 2.0)
    qi = l / (2.0 * qr)
    w = np.exp(-(qr + 1j * qi))
    g = b / (2.0 * r) * (qr - 1j * qi)

    def pack(t):
        t = t.reshape(2, H, N)
        return np.stack([t.real, t.imag], axis=1).astype(np.float32)

    source = np.stack([pack(np.conj(g * w ** (NZ - 1 - s))) for s in range(NZ)])
    return np.stack([pack(w), pack(g)]), source


def split(a):
    hi = a.astype(jnp.bfloat16)
    lo = (a - hi.astype(jnp.float32)).astype(jnp.bfloat16)
    return hi, lo


def dot_right(a, m_ref, q, exact=True):
    if not exact:
        return jnp.dot(a.astype(jnp.bfloat16), m_ref[q, 2], preferred_element_type=jnp.float32)
    hi, lo = split(a)
    mh, ml = m_ref[q, 0], m_ref[q, 1]
    return jnp.dot(
        jnp.concatenate([hi, lo, hi], axis=1),
        jnp.concatenate([mh, mh, ml], axis=0),
        preferred_element_type=jnp.float32,
    )


def dot_left(m_ref, q, a, exact=True):
    if not exact:
        return jnp.dot(m_ref[q, 2], a.astype(jnp.bfloat16), preferred_element_type=jnp.float32)
    hi, lo = split(a)
    mh, ml = m_ref[q, 0], m_ref[q, 1]
    return jnp.dot(
        jnp.concatenate([mh, mh, ml], axis=1),
        jnp.concatenate([hi, lo, hi], axis=0),
        preferred_element_type=jnp.float32,
    )


def forward_plane(re, im, right, left, store, exact=True):
    halves = []
    for q in (0, 1):
        if q == 0:
            a = jnp.concatenate([re[:, :H] + re[:, H:], im[:, :H] + im[:, H:]], axis=1)
        else:
            a = jnp.concatenate([re[:, :H] - re[:, H:], im[:, :H] - im[:, H:]], axis=1)
        halves.append(dot_right(a, right, q, exact))
    for q in (0, 1):
        parts = []
        for t in halves:
            u = t[:H] + t[H:] if q == 0 else t[:H] - t[H:]
            parts.append(jnp.concatenate([u[:, :H], u[:, H:]], axis=0))
        store(q, dot_left(left, q, jnp.concatenate(parts, axis=1), exact))


def inverse_plane(load, right, left):
    e = [dot_left(right, q, load(q)) for q in (0, 1)]
    e = [part * (1.0 / (N * N)) for part in e]
    top, bottom = e[0] + e[1], e[0] - e[1]
    re = jnp.concatenate([top[:H], bottom[:H]], axis=0)
    im = jnp.concatenate([top[H:], bottom[H:]], axis=0)
    e = []
    for q in (0, 1):
        z = jnp.concatenate([re[:, q * H : (q + 1) * H], im[:, q * H : (q + 1) * H]], axis=1)
        e.append(dot_right(z, left, q))
    low, high = e[0] + e[1], e[0] - e[1]
    re = jnp.concatenate([low[:, :H], high[:, :H]], axis=1)
    im = jnp.concatenate([low[:, H:], high[:, H:]], axis=1)
    return re, im


def cmul(a, b):
    return a[0] * b[0] - a[1] * b[1], a[0] * b[1] + a[1] * b[0]


def cadd(a, b):
    return a[0] + b[0], a[1] + b[1]


def csub(a, b):
    return a[0] - b[0], a[1] - b[1]


def tile_sum(a):
    a = a[:, :H] + a[:, H:]
    if a.shape[0] > 8:
        a = jnp.sum(a.reshape(a.shape[0] // 8, 8, H), axis=0)
    return a


def total_of(tile):
    return jnp.sum(jnp.sum(tile, axis=0, keepdims=True), axis=1, keepdims=True)


def kernel(
    angles_in, block, meas_in, dft_in, wg_in, source_table,
    fields, descent, misfit,
    angles, meas, dft, right, left, wg, inc, zbuf, c4, s_buf, f_buf, w_buf, gh0, gh1, g0, g1, r_buf, ybuf, red_out, red_in,
    mh, h7, part, rs_in, ar_out, ar_in,
    in_sem, ga_s, ga_r, gb_s, go_s, gb_r, x_s, x_r, rd_s, rd_r, pg_s, pg_r, ht_s, ht_r,
    rs_s, rs_r, a2_s, a2_r,
):
    illum = lax.axis_index("illum")
    slab = lax.axis_index("slab")
    chip = slab // 2
    core = slab - 2 * chip
    other = (illum, slab + 1 - 2 * core)

    x, z = illum // 8, lax.rem(illum, 8)

    def illum_at(dx, dz):
        return lax.rem(x + dx, 4) * 8 + lax.rem(z + dz, 8)

    def slab_peer(k):
        return (illum, lax.rem(slab + k, NZ))

    def sent(src, dst, s_sem, r_sem, dev):
        return pltpu.make_async_remote_copy(
            src_ref=src, dst_ref=dst, send_sem=s_sem, recv_sem=r_sem, device_id=dev, device_id_type=MESH
        )

    def wait_bytes(ref, sem):
        pltpu.make_async_copy(ref, ref, sem).wait()

    barrier = pltpu.get_barrier_semaphore()

    def greet(peer):
        pl.semaphore_signal(barrier, inc=1, device_id=peer, device_id_type=MESH)

    for dz in DEPTH_STEPS:
        greet((illum_at(0, dz), slab))
    for dx in (2, 1, 3):
        for k in range(4):
            greet((illum_at(dx, 0), 4 * core + k))
    for k in range(1, NZ):
        greet(slab_peer(k))

    loads = [
        pltpu.make_async_copy(src, dst, in_sem.at[i])
        for i, (src, dst) in enumerate((
            (angles_in, angles), (dft_in, dft), (meas_in, meas),
            (wg_in, wg), (source_table.at[slab], h7),
        ))
    ]
    for load in loads:
        load.start()
    pl.semaphore_wait(barrier, 7 + 12 + 7)

    high = slab // 4
    slot = slab + high * (7 - 2 * slab)

    def z_rows(k, n):
        return pl.ds(pl.multiple_of(k * n, n), n)

    def chip_peer(dx, dy):
        return (illum_at(dx, 0), 2 * lax.rem(chip + dy, 4) + high)

    for dz in DEPTH_STEPS:
        sent(block, zbuf.at[z_rows(z, 8)], ga_s, ga_r.at[z], (illum_at(0, dz), slab)).start()
    own_rows = pltpu.make_async_copy(block, zbuf.at[z_rows(z, 8)], ga_r.at[z])
    own_rows.start()

    def pass_on(step):
        k = lax.rem(z // 2 + 4 + step, 4)
        for i in (0, 1):
            pltpu.make_async_copy(block, zbuf.at[z_rows(2 * k + i, 8)], ga_r.at[2 * k + i]).wait()
        for dx, dy in EARLY_STEPS:
            rows = pl.ds(pl.multiple_of(x * 64 + k * 16, 16), 16)
            sent(zbuf.at[z_rows(k, 16)], c4.at[slot, rows], gb_s, gb_r.at[slot], chip_peer(dx, dy)).start()

    near = 2 * lax.rem(z, 2) - 1
    loads[0].wait()

    def angle_row(i):
        return jnp.sin(TILT * jnp.full((1, H), angles[0, i], jnp.int32).astype(jnp.float32))

    sine_x, sine_y = angle_row(0), angle_row(1)
    cos_z = jnp.sqrt(1.0 - sine_x * sine_x - sine_y * sine_y)
    x_at = lax.broadcasted_iota(jnp.int32, (N, H), 0).astype(jnp.float32)
    x_phase = WAVE * (sine_x * x_at)
    ex = jnp.cos(x_phase), jnp.sin(x_phase)
    y_at = lax.broadcasted_iota(jnp.int32, (1, H), 1).astype(jnp.float32)

    def incident(z):
        halves = []
        zf = jnp.full((1, H), z, jnp.int32).astype(jnp.float32)
        for q in (0, 1):
            phase = WAVE * (sine_y * (y_at + float(q * H)) + cos_z * zf)
            halves.append(cmul(ex, (jnp.cos(phase), jnp.sin(phase))))
        return tuple(jnp.concatenate([halves[0][i], halves[1][i]], axis=1) for i in (0, 1))

    def store_to(ref, p):
        def store(q, value):
            ref[p, q, 0] = value[:H]
            ref[p, q, 1] = value[H:]
        return store

    def load_from(ref, p):
        return lambda q: jnp.concatenate([ref[p, q, 0], ref[p, q, 1]], axis=0)

    def global_z(k):
        return k + core * (7 - 2 * k)

    def keep_incident(p):
        inc[p, 0], inc[p, 1] = incident(global_z(p))

    pl.loop(0, 4)(keep_incident)

    pass_on(0)
    pass_on(near)

    def store_mh(q, value):
        mh[q, 0] = value[:H]
        mh[q, 1] = value[H:]

    for load in loads[1:3]:
        load.wait()
    for q in (0, 1):
        for i, value in enumerate(split(dft[q])):
            right[q, i] = value
        for i, value in enumerate(split(dft[2 + q])):
            left[q, i] = value
        right[q, 2] = dft[4 + q].astype(jnp.bfloat16)
        left[q, 2] = dft[6 + q].astype(jnp.bfloat16)
    pass_on(-near)
    forward_plane(meas[0], meas[1], right, left, store_mh)
    pass_on(2)

    all_rows = pl.ds(pl.multiple_of(x * 64, 64), 64)
    for dx, dy in LATE_STEPS:
        sent(zbuf, c4.at[slot, all_rows], gb_s, gb_r.at[slot], chip_peer(dx, dy)).start()

    def to_other():
        return sent(zbuf, c4.at[slot, all_rows], go_s, gb_r.at[slot], other)

    @pl.when(core != high)
    def _():
        to_other().start()

    @pl.when(core == high)
    def _():
        c4[slot, all_rows] = zbuf[...]

    def wait_plane(k):
        here = (core == high) & (slot == k)

        @pl.when(here)
        def _():
            wait_bytes(c4.at[k, pl.ds(0, 192)], gb_r.at[k])

        @pl.when(jnp.logical_not(here))
        def _():
            wait_bytes(c4.at[k], gb_r.at[k])

    everything = slice(None)

    def pair(ref, *at, rows=everything):
        return ref[(*at, 0, rows)], ref[(*at, 1, rows)]

    def put(ref, value, *at, rows=everything):
        ref[(*at, 0, rows)] = value[0]
        ref[(*at, 1, rows)] = value[1]

    def table(t, xp, sign, rows=everything):
        re, im = pair(wg, t, xp, rows=rows)
        return re, im if sign > 0 else -im

    def chunks(n):
        size = H // 2 if n == 0 else H
        return [(xp, base, size) for xp in (0, 1) for base in range(0, H, size)]

    def exchange(n, q):
        xp, base, size = chunks(n)[q]
        rows = pl.ds(base, size)
        return sent(f_buf.at[2, xp, :, rows], ybuf.at[n, xp, :, rows], x_s.at[n, q], x_r.at[n, q], other)

    def forward_chained(p, re, im, n, exact=True):
        def store(q, value):
            v = value[:H], value[H:]
            put(s_buf, v, p, q)
            if p:
                before = pair(s_buf, 0, q) if p == 1 else pair(f_buf, p - 2, q)
                put(f_buf, cadd(v, cmul(table(0, q, 1), before)), p - 1, q)
            if p == 3:
                exchange(n, q).start()

        forward_plane(re, im, right, left, store, exact)

    first = 2 * lax.rem(chip + core, 2)
    for i in range(4):
        p = lax.rem(first + i, 4)
        wait_plane(p)
        c = c4[p]
        forward_plane(c * inc[p, 0], c * inc[p, 1], right, left, store_to(s_buf, p))
    loads[3].wait()
    for q, (xp, base, size) in enumerate(chunks(0)):

        @pl.loop(0, size // 16)
        def _(i):
            rows = pl.ds(pl.multiple_of(base + i * 16, 16), 16)
            w = table(0, xp, 1, rows)
            f = pair(s_buf, 0, xp, rows=rows)
            for k in range(1, 4):
                f = cadd(pair(s_buf, k, xp, rows=rows), cmul(w, f))
                put(f_buf, f, k - 1, xp, rows=rows)

        exchange(0, q).start()
    fields[0], fields[1] = incident(slab)

    def second_pass(src, n, sign, emit, acc):
        for q, (xp, base, size) in enumerate(chunks(n)):
            exchange(n, q).wait()

            def step(i, acc):
                rows = pl.ds(pl.multiple_of(base + i * 16, 16), 16)
                w, g = table(0, xp, sign, rows), table(1, xp, sign, rows)
                t = pair(ybuf, n, xp, rows=rows)
                out = [None] * 4
                for k in (3, 2, 1, 0):
                    u = cmul(w, t)
                    v = pair(src, k, xp, rows=rows)
                    f = v if k == 0 else pair(f_buf, k - 1, xp, rows=rows)
                    out[k] = cmul(g, cadd(f, u))
                    if k:
                        t = cadd(v, u)
                return emit(out, xp, rows, acc)

            acc = lax.fori_loop(0, size // 16, step, acc)
            if emit.following is not None and base + size == H:
                exchange(emit.following, xp).start()
        return acc

    def inverse_back(src, n, keep):
        for xp in (0, 1):
            exchange(n, xp).wait()
        for p in (3, 2, 1, 0):

            def load(q):
                u = cmul(table(0, q, -1), pair(ybuf, n, q))
                v = pair(src, p, q)
                f = v if p == 0 else pair(f_buf, p - 1, q)
                if p:
                    put(ybuf, cadd(v, u), n, q)
                return jnp.concatenate(cmul(table(1, q, -1), cadd(f, u)), axis=0)

            keep(p, *inverse_plane(load, right, left))

    zero = jnp.zeros((16, N), jnp.float32)

    def norm(acc, value):
        return acc + (value[0] * value[0] + value[1] * value[1])

    def reduce_start(n, rows):
        for i, tile in enumerate(rows):
            red_out[n, i] = tile
        used = pl.ds(0, len(rows))
        copy = sent(red_out.at[n, used], red_in.at[n, used], rd_s.at[n], rd_r.at[n], other)
        copy.start()
        return copy

    def forward_chain(values, w, xp, rows):
        f = values[0]
        for k in range(1, 4):
            f = cadd(values[k], cmul(w, f))
            put(f_buf, f, k - 1, xp, rows=rows)

    def emit_first(out, xp, rows, acc):
        for k in range(4):
            put(w_buf, out[k], k, xp, rows=rows)
        forward_chain(out, table(0, xp, -1, rows), xp, rows)
        return acc

    emit_first.following = 1

    second_pass(s_buf, 0, 1, emit_first, 0)

    for p in range(4):
        re, im = inverse_plane(load_from(w_buf, p), right, left)
        r_buf[p, 0] = re
        r_buf[p, 1] = im

    square_sums = []

    def keep_gradient(p, re, im):
        c = c4[p]
        re = r_buf[p, 0] - c * re
        im = r_buf[p, 1] - c * im
        g0[p, 0] = re
        g0[p, 1] = im
        square_sums.append(tile_sum(re * re + im * im))

    inverse_back(w_buf, 1, keep_gradient)
    zz0 = sum(square_sums)
    for p in range(4):
        c = c4[p]
        forward_chained(p, c * g0[p, 0], c * g0[p, 1], 2)

    sender = chip // 2
    send_index = 2 * chip + 1 + sender * (6 - 4 * chip)
    own_index = jnp.where(core == sender, 2 * chip + sender * (6 - 4 * chip), 4)

    def plane_copy(n, ref):
        return sent(ref.at[send_index], ref.at[4], pg_s.at[n], pg_r.at[n], other)

    def hat_copy():
        return sent(gh0.at[0], gh0.at[4], ht_s.at[0], ht_r.at[0], other)

    def last_copy():
        return sent(g1.at[0], g1.at[5], ht_s.at[1], ht_r.at[1], other)

    @pl.when(core == sender)
    def _():
        plane_copy(0, g0).start()

    for p in range(4):
        forward_plane(g0[p, 0], g0[p, 1], right, left, store_to(gh0, p))

    @pl.when(core == 1)
    def _():
        hat_copy().start()

    def emit_image(out, xp, rows, acc):
        image = []
        for k in range(4):
            m = csub(pair(gh0, k, xp, rows=rows), out[k])
            acc = norm(acc, m)
            put(w_buf, m, k, xp, rows=rows)
            image.append(m)
        forward_chain(image, table(0, xp, -1, rows), xp, rows)
        return acc

    emit_image.following = 3
    mm0 = second_pass(s_buf, 2, 1, emit_image, zero)
    red0 = reduce_start(0, (zz0, tile_sum(mm0)))

    for p in range(4):
        re, im = inverse_plane(load_from(w_buf, p), right, left)
        r_buf[p, 0] = re
        r_buf[p, 1] = im

    red0.wait()
    zz_first = total_of(red_out[0, 0] + red_in[0, 0])
    mm_first = total_of(red_out[0, 1] + red_in[0, 1]) * (1.0 / (N * N))
    alpha0 = zz_first / mm_first

    square_sums = []

    def keep_next(p, re, im):
        c = c4[p]
        re = g0[p, 0] - alpha0 * (r_buf[p, 0] - c * re)
        im = g0[p, 1] - alpha0 * (r_buf[p, 1] - c * im)
        g1[p, 0] = re
        g1[p, 1] = im
        square_sums.append(tile_sum(re * re + im * im))

    inverse_back(w_buf, 3, keep_next)
    red1 = reduce_start(1, (sum(square_sums),))
    for p in range(4):
        c = c4[p]
        forward_chained(p, c * g1[p, 0], c * g1[p, 1], 4, exact=False)

    @pl.when(core == sender)
    def _():
        plane_copy(1, g1).start()

    for p in range(4):
        forward_plane(g1[p, 0], g1[p, 1], right, left, store_to(gh1, p), exact=False)

    @pl.when(core == 1)
    def _():
        last_copy().start()

    red1.wait()
    zz_second = total_of(red_out[1, 0] + red_in[1, 0])
    beta0 = zz_second / zz_first

    def emit_last(out, xp, rows, acc):
        for k in range(4):
            m = csub(pair(gh1, k, xp, rows=rows), out[k])
            old = pair(w_buf, k, xp, rows=rows)
            acc = norm(acc, (m[0] + beta0 * old[0], m[1] + beta0 * old[1]))
        return acc

    emit_last.following = None
    mm1 = second_pass(s_buf, 4, 1, emit_last, zero)
    red2 = reduce_start(2, (tile_sum(mm1),))

    @pl.when(core == sender)
    def _():
        plane_copy(0, g0).wait_send()
        plane_copy(1, g1).wait_send()

    @pl.when(core != sender)
    def _():
        plane_copy(0, g0).wait_recv()
        plane_copy(1, g1).wait_recv()

    @pl.when(core == 1)
    def _():
        hat_copy().wait_send()
        last_copy().wait_send()

    @pl.when(core == 0)
    def _():
        hat_copy().wait_recv()
        last_copy().wait_recv()

    loads[4].wait()
    last = 5 * (1 - core)
    forward_plane(g1[last, 0], g1[last, 1], right, left, store_to(gh1, 4))
    red2.wait()
    mm_second = total_of(red_out[2, 0] + red_in[2, 0]) * (1.0 / (N * N))
    alpha1 = zz_second / mm_second
    weight0 = alpha0 + alpha1 * beta0

    hat = 4 * (1 - core)
    for xp in (0, 1):
        s7 = tuple(weight0 * gh0[hat, xp, i] + alpha1 * gh1[4, xp, i] - mh[xp, i] for i in (0, 1))
        back = cmul((h7[xp, 0], h7[xp, 1]), s7)
        w_buf[0, xp, 0] = back[0]
        w_buf[0, xp, 1] = back[1]
    back_re, back_im = inverse_plane(load_from(w_buf, 0), right, left)
    more_re = weight0 * g0[own_index, 0] + alpha1 * g1[own_index, 0]
    more_im = weight0 * g0[own_index, 1] + alpha1 * g1[own_index, 1]
    sol_re = fields[0] + more_re
    sol_im = fields[1] + more_im
    fields[0] = sol_re
    fields[1] = sol_im
    part[...] = sol_re * back_re + sol_im * back_im

    for dx, dz in ILLUM_STEPS:
        peer = illum_at(dx, dz)
        rows = pl.ds(pl.multiple_of(peer * 8, 8), 8)
        sent(part.at[rows], rs_in.at[illum], rs_s, rs_r, (peer, slab)).start()
    rs_in[illum] = part[pl.ds(pl.multiple_of(illum * 8, 8), 8), :]
    miss_re = more_re - meas[0]
    miss_im = more_im - meas[1]
    misfit_tile = tile_sum(miss_re * miss_re + miss_im * miss_im)
    is_last = jnp.where(slab == NZ - 1, 0.5, 0.0)
    misfit_row = is_last * jnp.sum(misfit_tile, axis=0, keepdims=True)
    wait_bytes(rs_in.at[pl.ds(0, ILLUMS - 1)], rs_r)

    rows = jnp.sum(rs_in[...], axis=0)
    square_row = jnp.sum(tile_sum(rows * rows), axis=0, keepdims=True)
    lane = lax.broadcasted_iota(jnp.int32, (1, H), 1)
    both = jnp.where(
        lane < H // 2,
        square_row + pltpu.roll(square_row, H // 2, 1),
        misfit_row + pltpu.roll(misfit_row, H // 2, 1),
    )
    ar_out[...] = both
    me = illum * NZ + slab
    for dx, dz, dy, dc in ALL_STEPS:
        peer = (illum_at(dx, dz), 2 * lax.rem(chip + dy, 4) + lax.rem(core + dc, 2))
        sent(ar_out, ar_in.at[pl.ds(me, 1)], a2_s, a2_r, peer).start()
    ar_in[pl.ds(me, 1)] = both
    wait_bytes(ar_in.at[pl.ds(0, DEVICES - 1)], a2_r)
    sums = jnp.sum(ar_in[...], axis=0, keepdims=True)
    square = jnp.sum(jnp.where(lane < H // 2, sums, 0.0), axis=1, keepdims=True)
    descent[...] = rows / jnp.sqrt(square * (1.0 / (NZ * N * N)) + 1e-06)
    misfit[0, 0] = jnp.sum(jnp.where(lane < H // 2, 0.0, sums))

    wait_bytes(zbuf.at[pl.ds(0, 56)], ga_s)

    @pl.when(core != high)
    def _():
        to_other().wait_send()

    for _ in range(15):
        wait_bytes(zbuf, gb_s)
    wait_bytes(rs_in.at[pl.ds(0, ILLUMS - 1)], rs_s)
    wait_bytes(ar_in.at[pl.ds(0, DEVICES - 1)], a2_s)


def body(angles, contrast, measured):
    dft = dft_tables()
    wg, source = depth_tables()
    vmem = pl.BlockSpec(memory_space=pltpu.VMEM)
    smem = pl.BlockSpec(memory_space=pltpu.SMEM)
    hbm = pl.BlockSpec(memory_space=pltpu.HBM)
    f32 = jnp.float32
    dma = pltpu.SemaphoreType.DMA
    spectral = (2, 2, H, N)
    fields, descent, misfit = pl.pallas_call(
        kernel,
        out_shape=(
            jax.ShapeDtypeStruct((2, N, N), f32),
            jax.ShapeDtypeStruct((8, N), f32),
            jax.ShapeDtypeStruct((1, 1), f32),
        ),
        in_specs=[hbm] * 6,
        out_specs=(vmem, vmem, smem),
        scratch_shapes=[
            pltpu.SMEM((1, 2), jnp.int32),
            pltpu.VMEM((2, N, N), f32),
            pltpu.VMEM((8, N, N), f32),
            pltpu.VMEM((2, 3, N, N), jnp.bfloat16),
            pltpu.VMEM((2, 3, N, N), jnp.bfloat16),
            pltpu.VMEM((2, *spectral), f32),
            pltpu.VMEM((4, 2, N, N), f32),
            pltpu.VMEM((64, N), f32),
            pltpu.VMEM((4, N, N), f32),
            pltpu.VMEM((4, *spectral), f32),
            pltpu.VMEM((3, *spectral), f32),
            pltpu.VMEM((4, *spectral), f32),
            pltpu.VMEM((5, *spectral), f32),
            pltpu.VMEM((5, *spectral), f32),
            pltpu.VMEM((5, 2, N, N), f32),
            pltpu.VMEM((6, 2, N, N), f32),
            pltpu.VMEM((4, 2, N, N), f32),
            pltpu.VMEM((5, *spectral), f32),
            pltpu.VMEM((3, 2, 8, H), f32),
            pltpu.VMEM((3, 2, 8, H), f32),
            pltpu.VMEM(spectral, f32),
            pltpu.VMEM(spectral, f32),
            pltpu.VMEM((N, N), f32),
            pltpu.VMEM((ILLUMS, 8, N), f32),
            pltpu.VMEM((1, H), f32),
            pltpu.VMEM((DEVICES, H), f32),
            dma((5,)), dma, dma((8,)), dma, dma, dma((4,)),
            dma((5, 4)), dma((5, 4)),
            dma((3,)), dma((3,)), dma((2,)), dma((2,)), dma((2,)), dma((2,)),
            dma, dma, dma, dma,
        ],
        compiler_params=pltpu.CompilerParams(
            collective_id=0, has_side_effects=True, vmem_limit_bytes=53 * 1024 * 1024,
        ),
    )(
        angles, contrast.reshape(8, N), measured.reshape(2, N, N),
        jnp.asarray(dft), jnp.asarray(wg), jnp.asarray(source),
    )
    return fields.reshape(1, 2, 1, N, N), descent.reshape(1, 8, N), misfit.reshape(())


def solution(mesh):
    return jax.shard_map(
        body,
        mesh=mesh,
        in_specs=(P("illum", None), P("slab", "illum", None), P("illum", None, None, None)),
        out_specs=(P("illum", None, "slab", None, None), P("slab", "illum", None), P()),
        check_vma=False,
    )
```
